32 devices in a mesh: groups: 2 (over x), eig: 16 (over z, y, core).
Axes of the slice: x: 2, y: 2, z: 4, core: 2. Of those that a mesh axis runs over, the one named last changes fastest.
Arguments:
- features: bfloat16 [1024, 32768], P(None, 'eig'), may hold values from -0.1875 to 0.1875
- responses: bfloat16 [1024, 2048], P(None, 'groups'), parts along dimension 1, may hold values from -6 to 6
- basis: bfloat16 [32768, 256], P('eig'), may hold values from -0.25 to 0.25
- eigenvalues: float32 [256], replicated, may hold values from 0.2 to 20
- reg_index: int32 [2048], P('groups'), parts along dimension 0, may hold values from 0 to 15
- subject: int32 [2048], P('groups'), parts along dimension 0, may hold values from 0 to 7
- alpha_table: float32 [8, 16], replicated, may hold values from 0.1 to 10
Outputs:
- weights: bfloat16 [32768, 2048], P('eig', 'groups'), parts along dimension 1
The draws below stay inside these ranges and needn't reach their ends.
There are 2 independent parts, one for each index of `groups`. The reference program is written for one: setup_inputs(seed, part) draws one part's arguments, and reference() takes and returns one part's arrays. A program takes and returns all parts, laid end to end along the dimension named above; an argument that names none is the same for every part. Nothing has to cross between parts.
All inputs are finite; a program needn't handle non-finite values.
Results may differ from the reference program's by a relative error of at most 0.0049.
Values may be sent and summed in bfloat16 or wider, within the bound.
No kernel may reach another device: no remote copies, remote signals or barrier semaphores. Data moves between devices by JAX's collectives and lax.ppermute only.
A program may use at most 64 MiB of HBM per device.

```python
import math
import jax
import jax.numpy as jnp
import numpy as np
from jax import lax

P_SIZE = 32768
K = 256
VOX = 1024
TIMES = 1024
SUBJECTS = 8
GRID = 16


def place_ends(drawn, key, least, largest):
    place = [jax.random.randint(jax.random.fold_in(key, axis), (), 0, length) for axis, length in enumerate(drawn.shape)]
    longest = drawn.shape.index(max(drawn.shape))
    beside = place[:longest] + [(place[longest] + 1) % drawn.shape[longest]] + place[longest + 1:]
    return drawn.at[tuple(place)].set(least).at[tuple(beside)].set(largest)


def spiked(result, key, source, target, parts, factor):
    def block_of(dim):
        return (jnp.arange(result.shape[dim]) // (result.shape[dim] // parts)).reshape((-1,) + (1,) * (result.ndim - 1 - dim))

    near = jax.random.permutation(key, parts)[block_of(target)]
    far = (block_of(target) + parts // 2) % parts
    return jnp.where((block_of(source) == near) | (block_of(source) == far), factor * result, result)


def block_scale(own_key, extent, shards, smallest, largest):
    def one(axis_at, parts):
        draws = jax.random.uniform(jax.random.fold_in(jax.random.fold_in(own_key, 6), axis_at), (parts,), jnp.float32, smallest / len(shards), largest / len(shards))
        return jnp.repeat(jnp.exp(draws), extent[axis_at] // parts).reshape((-1,) + (1,) * (len(extent) - axis_at - 1))

    level = one(*shards[0])
    for cut in shards[1:]:
        level = level * one(*cut)
    return level


def rank_table(amount, skew):
    weights = [(1 << 20) // math.isqrt(rank ** skew) + 1 for rank in range(1, amount + 1)]
    spread = 1 + sum(weights) // (1 << 30)
    return np.cumsum(np.array([max(1, weight // spread) for weight in weights]))


def ranked(key, dims, count, lean):
    listing = rank_table(count, lean)
    pick = jax.random.randint(jax.random.fold_in(key, 1), dims, 0, int(listing[count - 1]))
    rank = jnp.searchsorted(jnp.asarray(listing, jnp.int32), pick, side="right")
    return jax.random.permutation(jax.random.fold_in(key, 2), count)[rank].astype(jnp.int32)


def centred(rng, extent, width, bound, split=(), dtype=jnp.bfloat16):
    result = width * jax.random.normal(rng, extent, jnp.float32)
    if split:
        result = result * block_scale(rng, extent, split, -0.22, 0.18)
    return jnp.clip(result, -bound, bound).astype(dtype)


def noise_with(key, dims, spread, bound, split, heavy, held_as=jnp.bfloat16):
    drawn = spread * jax.random.normal(key, dims, jnp.float32)
    if split:
        drawn = drawn * block_scale(key, dims, split, -0.22, 0.18)
    return jnp.clip(spiked(drawn, jax.random.fold_in(key, 3), *heavy), -bound, bound).astype(held_as)


def setup_inputs(seed: int = 0, part: int = 0) -> dict:
    keys = jax.random.split(jax.random.key(seed), 8)
    part_splits = jax.random.split(jax.random.fold_in(keys[7], part), 8)
    return {
        "features": centred(keys[0], (TIMES, P_SIZE), TIMES ** -0.5, 0.1875, ((1, 16),)),
        "responses": centred(part_splits[1], (TIMES, VOX), 1.0, 6.0),
        "basis": noise_with(keys[2], (P_SIZE, K), (4 * K) ** -0.5, 0.25, ((0, 16),), (0, 1, 16, 2.0)),
        "eigenvalues": jnp.clip(jnp.exp(jax.random.uniform(keys[3], (K,), jnp.float32, math.log(0.2), math.log(20.0))), 0.2, 20.0),
        "reg_index": place_ends(jax.random.randint(part_splits[4], (VOX,), 0, GRID), jax.random.fold_in(part_splits[4], 1), 0, GRID - 1).astype(jnp.int32),
        "subject": place_ends(ranked(part_splits[5], (VOX,), SUBJECTS, 2), jax.random.fold_in(part_splits[5], 3), 0, SUBJECTS - 1).astype(jnp.int32),
        "alpha_table": jnp.clip(jnp.exp(jax.random.uniform(keys[6], (SUBJECTS, GRID), jnp.float32, math.log(0.1), math.log(10.0))), 0.1, 10.0),
    }


def reference(features, responses, basis, eigenvalues, reg_index, subject, alpha_table):
    cross = jnp.dot(features.T, responses, preferred_element_type=jnp.float32)
    spectrum = jnp.dot(basis.T.astype(jnp.float32), cross, precision=lax.Precision.HIGHEST)
    alpha = alpha_table[subject, reg_index]
    scaled = (spectrum / (eigenvalues[:, None] + alpha[None, :])).astype(jnp.bfloat16)
    weights = jnp.dot(basis, scaled, preferred_element_type=jnp.float32)
    return weights.astype(jnp.bfloat16)
```

```python
import functools

import jax
import jax.numpy as jnp
from jax import lax
from jax.experimental import pallas as pl
from jax.experimental.pallas import tpu as pltpu
from jax.sharding import PartitionSpec as P

F32 = jnp.float32
BF16 = jnp.bfloat16


def lookup_alpha(reg_index, subject, alpha_table):
    subjects, grid = alpha_table.shape
    flat_codes = subject * grid + reg_index
    codes = jnp.arange(subjects * grid, dtype=jnp.int32)
    matches = flat_codes[:, None] == codes[None, :]
    table_row = alpha_table.reshape(-1)[None, :]
    return jnp.sum(jnp.where(matches, table_row, 0.0), axis=1)


def gram_kernel(steps, place_ref, f_ref, b_ref, own_ref, send_ref, acc_ref):
    i = pl.program_id(0)
    core = place_ref[1]
    half = own_ref.shape[1]

    @pl.when(i == 0)
    def _():
        acc_ref[...] = jnp.zeros_like(acc_ref)

    acc_ref[...] += jnp.dot(f_ref[...], b_ref[...], preferred_element_type=F32)

    @pl.when(i == steps - 1)
    def _():
        low, high = acc_ref[:, :half], acc_ref[:, half:]
        first = core == 0
        own_ref[...] = jnp.where(first, low, high)
        send_ref[...] = jnp.where(first, high, low).astype(BF16)


def gram(place, features, basis, groups):
    times, feats = features.shape
    k = basis.shape[1]
    rows = times // groups
    chunk = min(512, feats)
    steps = feats // chunk
    return pl.pallas_call(
        functools.partial(gram_kernel, steps),
        grid_spec=pltpu.PrefetchScalarGridSpec(
            num_scalar_prefetch=1,
            grid=(steps,),
            in_specs=[
                pl.BlockSpec((rows, chunk), lambda i, place: (place[0], i)),
                pl.BlockSpec((chunk, k), lambda i, place: (i, 0)),
            ],
            out_specs=[
                pl.BlockSpec((rows, k // 2), lambda i, place: (0, 0)),
                pl.BlockSpec((rows, k // 2), lambda i, place: (0, 0)),
            ],
            scratch_shapes=[pltpu.VMEM((rows, k), F32)],
        ),
        out_shape=[
            jax.ShapeDtypeStruct((rows, k // 2), F32),
            jax.ShapeDtypeStruct((rows, k // 2), BF16),
        ],
        name="gram",
    )(place, features, basis)


def spectrum_kernel(pieces, place_ref, *refs):
    piece_refs = refs[:pieces]
    r_ref, eig_ref, alpha_ref, out_ref = refs[pieces:]
    group = place_ref[0]
    rows = piece_refs[0].shape[0]
    total = jnp.zeros(out_ref.shape, F32)
    for m, piece in enumerate(piece_refs):
        start = pl.multiple_of((group ^ m) * rows, rows)
        total += lax.dot_general(
            piece[...].astype(BF16),
            r_ref[pl.ds(start, rows), :],
            (((0,), (0,)), ((), ())),
            preferred_element_type=F32,
        )
    out_ref[...] = (total / (eig_ref[...] + alpha_ref[...])).astype(BF16)


def spectrum(place, pieces, responses, eig_column, alpha_row):
    half = pieces[0].shape[1]
    vmem = pl.BlockSpec(memory_space=pltpu.VMEM)
    return pl.pallas_call(
        functools.partial(spectrum_kernel, len(pieces)),
        in_specs=[pl.BlockSpec(memory_space=pltpu.SMEM)] + [vmem] * (len(pieces) + 3),
        out_specs=vmem,
        out_shape=jax.ShapeDtypeStruct((half, responses.shape[1]), BF16),
        name="spectrum",
    )(place, *pieces, responses, eig_column, alpha_row)


def weights_kernel(place_ref, b_ref, own_ref, got_ref, out_ref):
    first = place_ref[1] == 0
    own, got = own_ref[...], got_ref[...]
    low = jnp.where(first, own, got)
    high = jnp.where(first, got, own)
    scaled = jnp.concatenate([low, high], axis=0)
    out_ref[...] = jnp.dot(b_ref[...], scaled, preferred_element_type=F32).astype(BF16)


def weights(place, basis, own, got):
    feats, k = basis.shape
    half, vox = own.shape
    chunk = min(256, feats)
    return pl.pallas_call(
        weights_kernel,
        grid_spec=pltpu.PrefetchScalarGridSpec(
            num_scalar_prefetch=1,
            grid=(feats // chunk,),
            in_specs=[
                pl.BlockSpec((chunk, k), lambda i, place: (i, 0)),
                pl.BlockSpec((half, vox), lambda i, place: (0, 0)),
                pl.BlockSpec((half, vox), lambda i, place: (0, 0)),
            ],
            out_specs=pl.BlockSpec((chunk, vox), lambda i, place: (i, 0)),
        ),
        out_shape=jax.ShapeDtypeStruct((feats, vox), BF16),
        name="weights",
    )(place, basis, own, got)


def swap(value, axis, bit):
    size = lax.axis_size(axis)
    return lax.ppermute(value, axis, [(i, i ^ bit) for i in range(size)])


def bits(size):
    out = []
    while (1 << len(out)) < size:
        out.append(1 << len(out))
    return out


def body(features, responses, basis, eigenvalues, reg_index, subject, alpha_table):
    groups = lax.axis_size("groups")
    group, eig = lax.axis_index("groups"), lax.axis_index("eig")
    core = eig & 1
    place = jnp.stack([group, core]).astype(jnp.int32)
    half = basis.shape[1] // 2

    alpha = lookup_alpha(reg_index, subject, alpha_table)[None, :]
    eig_column = lax.dynamic_slice_in_dim(eigenvalues, core * half, half, 0)[:, None]

    total, send = gram(place, features, basis, groups)
    total = total + swap(send, "eig", 1).astype(F32)
    for bit in bits(lax.axis_size("eig"))[1:]:
        total = total + swap(total.astype(BF16), "eig", bit).astype(F32)

    pieces = [total.astype(BF16)]
    for bit in bits(groups):
        pieces = pieces + [swap(piece, "groups", bit) for piece in pieces]
    own = spectrum(place, pieces, responses, eig_column, alpha)
    got = swap(own, "eig", 1)
    return weights(place, basis, own, got)


def solution(mesh):
    in_specs = (
        P(None, "eig"),
        P(None, "groups"),
        P("eig", None),
        P(),
        P("groups"),
        P("groups"),
        P(),
    )
    out_specs = P("eig", "groups")
    return jax.shard_map(body, mesh=mesh, in_specs=in_specs, out_specs=out_specs, check_vma=False)
```

```python
import functools

import jax
import jax.numpy as jnp
from jax import lax
from jax.experimental import pallas as pl
from jax.experimental.pallas import tpu as pltpu
from jax.sharding import PartitionSpec as P

F32 = jnp.float32
BF16 = jnp.bfloat16
MIB = 1 << 20
VMEM = pl.BlockSpec(memory_space=pltpu.VMEM)
SMEM = pl.BlockSpec(memory_space=pltpu.SMEM)
HBM = pl.BlockSpec(memory_space=pltpu.HBM)


def params(mib):
    return pltpu.CompilerParams(vmem_limit_bytes=mib * MIB)


def cost(flops, moved):
    return pl.CostEstimate(flops=flops, bytes_accessed=moved, transcendentals=0)


def core_index():
    return lax.axis_index("eig") & 1


def gram_kernel(f_hbm, b_hbm, own_ref, send_ref, f_ref, b_ref, f_sem, b_sem):
    rows, feats = f_ref.shape
    half = own_ref.shape[1]
    parts = f_sem.shape[0]
    chunk = feats // parts
    first_row = pl.multiple_of(lax.axis_index("groups") * rows, rows)
    copies = []
    for i in range(parts):
        cols = pl.ds(i * chunk, chunk)
        b_copy = pltpu.make_async_copy(b_hbm.at[cols], b_ref.at[cols], b_sem.at[i])
        f_copy = pltpu.make_async_copy(
            f_hbm.at[pl.ds(first_row, rows), cols], f_ref.at[:, cols], f_sem.at[i]
        )
        b_copy.start()
        f_copy.start()
        copies.append((b_copy, f_copy))
    total = None
    for i, (b_copy, f_copy) in enumerate(copies):
        cols = pl.ds(i * chunk, chunk)
        b_copy.wait()
        f_copy.wait()
        term = jnp.dot(f_ref[:, cols], b_ref[cols, :], preferred_element_type=F32)
        total = term if total is None else total + term
    low, high = total[:, :half], total[:, half:]
    first = core_index() == 0
    own_ref[...] = jnp.where(first, low, high)
    send_ref[...] = jnp.where(first, high, low).astype(BF16)


def gram(features, basis, groups):
    times, feats = features.shape
    k = basis.shape[1]
    rows = times // groups
    parts = 2
    return pl.pallas_call(
        gram_kernel,
        in_specs=[HBM, HBM],
        out_specs=[VMEM, VMEM],
        out_shape=[
            jax.ShapeDtypeStruct((rows, k // 2), F32),
            jax.ShapeDtypeStruct((rows, k // 2), BF16),
        ],
        scratch_shapes=[
            pltpu.VMEM((rows, feats), BF16),
            pltpu.VMEM((feats, k), BF16),
            pltpu.SemaphoreType.DMA((parts,)),
            pltpu.SemaphoreType.DMA((parts,)),
        ],
        compiler_params=params(12),
        cost_estimate=cost(2 * rows * feats * k, 2 * (rows + k) * feats),
        name="gram",
    )(features, basis)


def inverse_kernel(table_ref, reg_ref, subject_ref, eig_ref, out_ref):
    subjects, grid = table_ref.shape
    half = out_ref.shape[0]
    code = subject_ref[...] * grid + reg_ref[...]
    alpha = jnp.zeros(code.shape, F32)
    for s in range(subjects):
        for g in range(grid):
            alpha = jnp.where(code == s * grid + g, table_ref[s, g], alpha)
    eig_row = jnp.where(core_index() == 0, eig_ref[:, :half], eig_ref[:, half:])
    shape = (half, half)
    diagonal = lax.broadcasted_iota(jnp.int32, shape, 0) == lax.broadcasted_iota(jnp.int32, shape, 1)
    eig_column = jnp.sum(jnp.where(diagonal, eig_row, 0.0), axis=1, keepdims=True)
    out_ref[...] = 1.0 / (eig_column + alpha)


def inverse(alpha_table, reg_index, subject, eigenvalues):
    vox = reg_index.shape[0]
    k = eigenvalues.shape[0]
    return pl.pallas_call(
        inverse_kernel,
        in_specs=[SMEM, VMEM, VMEM, VMEM],
        out_specs=VMEM,
        out_shape=jax.ShapeDtypeStruct((k // 2, vox), F32),
        compiler_params=params(8),
        cost_estimate=cost(8 * k * vox, 2 * k * vox),
        name="inverse",
    )(alpha_table, reg_index[None, :], subject[None, :], eigenvalues[None, :])


def times_of(piece, r_ref, place):
    rows = piece.shape[0]
    start = pl.multiple_of(place * rows, rows)
    return lax.dot_general(
        piece[...], r_ref[pl.ds(start, rows), :], (((0,), (0,)), ((), ())), preferred_element_type=F32
    )


def share_kernel(piece_ref, r_ref, out_ref):
    out_ref[...] = times_of(piece_ref, r_ref, lax.axis_index("groups"))


def share(piece, responses):
    rows, half = piece.shape
    vox = responses.shape[1]
    return pl.pallas_call(
        share_kernel,
        in_specs=[VMEM, VMEM],
        out_specs=VMEM,
        out_shape=jax.ShapeDtypeStruct((half, vox), F32),
        compiler_params=params(8),
        cost_estimate=cost(2 * rows * half * vox, 2 * rows * vox),
        name="share",
    )(piece, responses)


def scale_kernel(pieces, *refs):
    part_ref, inverse_ref, r_ref, out_ref = refs[pieces:]
    group = lax.axis_index("groups")
    total = part_ref[...]
    for m in range(pieces):
        total += times_of(refs[m], r_ref, group ^ (m + 1))
    out_ref[...] = (total * inverse_ref[...]).astype(BF16)


def scale(part, pieces, inv, responses):
    half, vox = part.shape
    rows = responses.shape[0]
    return pl.pallas_call(
        functools.partial(scale_kernel, len(pieces)),
        in_specs=[VMEM] * (len(pieces) + 3),
        out_specs=VMEM,
        out_shape=jax.ShapeDtypeStruct((half, vox), BF16),
        compiler_params=params(8),
        cost_estimate=cost(2 * rows * half * vox, 2 * rows * vox),
        name="scale",
    )(*pieces, part, inv, responses)


def weights_kernel(b_ref, own_ref, got_ref, out_hbm, s_ref, out_ref, sems):
    parts = sems.shape[0]
    half, vox = own_ref.shape
    first = core_index() == 0
    own, got = own_ref[...], got_ref[...]
    s_ref[:half, :] = jnp.where(first, own, got)
    s_ref[half:, :] = jnp.where(first, got, own)
    chunk = vox // parts
    copies = []
    for i in range(parts):
        cols = pl.ds(i * chunk, chunk)
        out_ref[:, cols] = jnp.dot(b_ref[...], s_ref[:, cols], preferred_element_type=F32).astype(BF16)
        copy = pltpu.make_async_copy(out_ref.at[:, cols], out_hbm.at[:, cols], sems.at[i])
        copy.start()
        copies.append(copy)
    for copy in copies:
        copy.wait()


def weights(basis, own, got):
    feats, k = basis.shape
    half, vox = own.shape
    parts = 4
    return pl.pallas_call(
        weights_kernel,
        in_specs=[VMEM, VMEM, VMEM],
        out_specs=HBM,
        out_shape=jax.ShapeDtypeStruct((feats, vox), BF16),
        scratch_shapes=[
            pltpu.VMEM((k, vox), BF16),
            pltpu.VMEM((feats, vox), BF16),
            pltpu.SemaphoreType.DMA((parts,)),
        ],
        compiler_params=params(16),
        cost_estimate=cost(2 * feats * k * vox, 2 * feats * vox),
        name="weights",
    )(basis, own, got)


def swap(value, axis, bit):
    size = lax.axis_size(axis)
    return lax.ppermute(value, axis, [(i, i ^ bit) for i in range(size)])


def bits(size):
    out = []
    while (1 << len(out)) < size:
        out.append(1 << len(out))
    return out


def body(features, responses, basis, eigenvalues, reg_index, subject, alpha_table):
    groups = lax.axis_size("groups")
    total, send = gram(features, basis, groups)
    total = total + swap(send, "eig", 1).astype(F32)
    for bit in bits(lax.axis_size("eig"))[1:]:
        total = total + swap(total.astype(BF16), "eig", bit).astype(F32)

    pieces = [total.astype(BF16)]
    for bit in bits(groups):
        pieces = pieces + [swap(piece, "groups", bit) for piece in pieces]
    part = share(pieces[0], responses)
    inv = inverse(alpha_table, reg_index, subject, eigenvalues)
    own = scale(part, pieces[1:], inv, responses)
    got = swap(own, "eig", 1)
    return weights(basis, own, got)


def solution(mesh):
    in_specs = (
        P(None, "eig"),
        P(None, "groups"),
        P("eig", None),
        P(),
        P("groups"),
        P("groups"),
        P(),
    )
    out_specs = P("eig", "groups")
    return jax.shard_map(body, mesh=mesh, in_specs=in_specs, out_specs=out_specs, check_vma=False)
```

```python
import functools

import jax
import jax.numpy as jnp
from jax import lax
from jax.experimental import pallas as pl
from jax.experimental.pallas import tpu as pltpu
from jax.sharding import PartitionSpec as P

F32 = jnp.float32
BF16 = jnp.bfloat16
MIB = 1 << 20
CHAINS = 2
ANY = pl.BlockSpec(memory_space=pl.ANY)
HBM = pl.BlockSpec(memory_space=pltpu.HBM)
VMEM = pl.BlockSpec(memory_space=pltpu.VMEM)
SMEM = pl.BlockSpec(memory_space=pltpu.SMEM)


def params(mib):
    return pltpu.CompilerParams(vmem_limit_bytes=mib * MIB)


def cost(flops, moved):
    return pl.CostEstimate(flops=flops, bytes_accessed=moved, transcendentals=0)


def in_hbm(value):
    return pltpu.with_memory_space_constraint(value, pltpu.HBM)


def core_index():
    return lax.axis_index("eig") & 1


def gram_kernel(f_hbm, b_hbm, *refs):
    *outs, f_ref, b_ref, f_sem, b_sem = refs
    totals, sends = outs[:CHAINS], outs[CHAINS:]
    rows, feats = f_ref.shape
    half = b_ref.shape[1] // 2
    parts = f_sem.shape[0]
    chunk = feats // parts
    first_row = pl.multiple_of(lax.axis_index("groups") * rows, rows)
    copies = []
    for i in range(parts):
        cols = pl.ds(i * chunk, chunk)
        b_copy = pltpu.make_async_copy(b_hbm.at[cols], b_ref.at[cols], b_sem.at[i])
        f_copy = pltpu.make_async_copy(
            f_hbm.at[pl.ds(first_row, rows), cols], f_ref.at[:, cols], f_sem.at[i]
        )
        b_copy.start()
        f_copy.start()
        copies.append((b_copy, f_copy))
    total = None
    for i, (b_copy, f_copy) in enumerate(copies):
        cols = pl.ds(i * chunk, chunk)
        b_copy.wait()
        f_copy.wait()
        term = jnp.dot(f_ref[:, cols], b_ref[cols, :], preferred_element_type=F32)
        total = term if total is None else total + term
    low, high = total[:, :half], total[:, half:]
    first = core_index() == 0
    kept = jnp.where(first, low, high)
    sent = jnp.where(first, high, low).astype(BF16)
    size = rows // CHAINS
    for i in range(CHAINS):
        totals[i][...] = kept[i * size : (i + 1) * size]
        sends[i][...] = sent[i * size : (i + 1) * size]


def gram(features, basis, groups):
    times, feats = features.shape
    k = basis.shape[1]
    rows = times // groups
    parts = 2
    out = [
        jax.ShapeDtypeStruct((rows // CHAINS, k // 2), dtype) for dtype in (F32, BF16) for _ in range(CHAINS)
    ]
    result = pl.pallas_call(
        gram_kernel,
        in_specs=[HBM, HBM],
        out_specs=[VMEM] * len(out),
        out_shape=out,
        scratch_shapes=[
            pltpu.VMEM((rows, feats), BF16),
            pltpu.VMEM((feats, k), BF16),
            pltpu.SemaphoreType.DMA((parts,)),
            pltpu.SemaphoreType.DMA((parts,)),
        ],
        compiler_params=params(12),
        cost_estimate=cost(2 * rows * feats * k, 2 * (rows + k) * feats),
        name="gram",
    )(in_hbm(features), in_hbm(basis))
    return list(result[:CHAINS]), list(result[CHAINS:])


def inverse_kernel(table_ref, reg_ref, subject_ref, eig_ref, *refs):
    out_ref = refs[-1]
    subjects, grid = table_ref.shape
    k = out_ref.shape[0]
    code = subject_ref[...] * grid + reg_ref[...]
    alpha = jnp.zeros(code.shape, F32)
    for s in range(subjects):
        for g in range(grid):
            alpha = jnp.where(code == s * grid + g, table_ref[s, g], alpha)
    side = min(k, 128)
    first = core_index() == 0
    eig = jnp.where(first, eig_ref[:, :k], eig_ref[:, k:])
    shape = (side, side)
    diagonal = lax.broadcasted_iota(jnp.int32, shape, 0) == lax.broadcasted_iota(jnp.int32, shape, 1)
    for i in range(k // side):
        at = pl.ds(i * side, side)
        column = jnp.sum(jnp.where(diagonal, eig[:, i * side : (i + 1) * side], 0.0), axis=1, keepdims=True)
        out_ref[at, :] = 1.0 / (column + alpha)


def inverse(alpha_table, reg_index, subject, eigenvalues, after):
    vox = reg_index.shape[0]
    k = eigenvalues.shape[0] // 2
    return pl.pallas_call(
        inverse_kernel,
        in_specs=[SMEM, VMEM, VMEM, VMEM] + [ANY] * len(after),
        out_specs=VMEM,
        out_shape=jax.ShapeDtypeStruct((k, vox), F32),
        compiler_params=params(8),
        cost_estimate=cost(8 * k * vox, 2 * k * vox),
        name="inverse",
    )(alpha_table, reg_index[None, :], subject[None, :], eigenvalues[None, :], *after)


def add_kernel(total_ref, got_ref, *refs):
    out_ref, send_ref = refs[-2:]
    total = total_ref[...] + got_ref[...].astype(F32)
    out_ref[...] = total
    send_ref[...] = total.astype(BF16)


def add_last_kernel(total_ref, got_ref, *refs):
    refs[-1][...] = (total_ref[...] + got_ref[...].astype(F32)).astype(BF16)


def add(total, got, after, last=False):
    shape = total.shape
    both = [jax.ShapeDtypeStruct(shape, F32), jax.ShapeDtypeStruct(shape, BF16)]
    return pl.pallas_call(
        add_last_kernel if last else add_kernel,
        in_specs=[VMEM, VMEM] + [ANY] * len(after),
        out_specs=VMEM if last else [VMEM, VMEM],
        out_shape=both[1] if last else both,
        compiler_params=params(4),
        cost_estimate=cost(total.size, 12 * total.size),
        name="add",
    )(total, got, *after)


def share_kernel(places, has_sum, finish, *refs):
    n = len(places)
    r_ref, out_ref = refs[n], refs[-1]
    rest = list(refs[n + 1 : -1])
    group = lax.axis_index("groups")
    total = rest.pop(0)[...] if has_sum else None
    for (m, at), piece in zip(places, refs):
        rows = piece.shape[0]
        start = pl.multiple_of(((group ^ m) * CHAINS + at) * rows, rows)
        term = lax.dot_general(
            piece[...], r_ref[pl.ds(start, rows), :], (((0,), (0,)), ((), ())), preferred_element_type=F32
        )
        total = term if total is None else total + term
    if finish:
        total = total * rest.pop(0)[...]
    out_ref[...] = total.astype(out_ref.dtype)


def share(places, pieces, responses, before=None, inv=None):
    rows, k = pieces[0].shape
    vox = responses.shape[1]
    extra = [value for value in (before, inv) if value is not None]
    return pl.pallas_call(
        functools.partial(share_kernel, places, before is not None, inv is not None),
        in_specs=[VMEM] * (len(pieces) + 1 + len(extra)),
        out_specs=VMEM,
        out_shape=jax.ShapeDtypeStruct((k, vox), F32 if inv is None else BF16),
        compiler_params=params(8),
        cost_estimate=cost(2 * len(places) * rows * k * vox, 2 * rows * vox),
        name="share",
    )(*pieces, responses, *extra)


def weights_kernel(b_ref, own_ref, got_ref, out_hbm, s_ref, out_ref, sems):
    parts = sems.shape[0]
    half = own_ref.shape[0]
    first = core_index() == 0
    own, got = own_ref[...], got_ref[...]
    s_ref[:half, :] = jnp.where(first, own, got)
    s_ref[half:, :] = jnp.where(first, got, own)
    chunk = b_ref.shape[0] // parts
    copies = []
    for i in range(parts):
        rows = pl.ds(i * chunk, chunk)
        out_ref[rows, :] = jnp.dot(b_ref[rows, :], s_ref[...], preferred_element_type=F32).astype(BF16)
        copy = pltpu.make_async_copy(out_ref.at[rows], out_hbm.at[rows], sems.at[i])
        copy.start()
        copies.append(copy)
    for copy in copies:
        copy.wait()


def weights(basis, own, got):
    feats, k = basis.shape
    half, vox = own.shape
    parts = 8
    return pl.pallas_call(
        weights_kernel,
        in_specs=[VMEM, VMEM, VMEM],
        out_specs=HBM,
        out_shape=jax.ShapeDtypeStruct((feats, vox), BF16),
        scratch_shapes=[
            pltpu.VMEM((k, vox), BF16),
            pltpu.VMEM((feats, vox), BF16),
            pltpu.SemaphoreType.DMA((parts,)),
        ],
        compiler_params=params(16),
        cost_estimate=cost(2 * feats * k * vox, 2 * feats * vox),
        name="weights",
    )(basis, own, got)


def swap(value, axis, mask):
    return lax.ppermute(value, axis, [(i, i ^ mask) for i in range(lax.axis_size(axis))])


def bits(size):
    out = []
    while (1 << len(out)) < size:
        out.append(1 << len(out))
    return out


def orders(size):
    steps = bits(size)[1:]
    return [steps, steps[1:] + steps[:1]]


def body(features, responses, basis, eigenvalues, reg_index, subject, alpha_table):
    groups = lax.axis_size("groups")
    totals, sends = gram(features, basis, groups)
    gots = [swap(send, "eig", 1) for send in sends]
    inv = inverse(alpha_table, reg_index, subject, eigenvalues, tuple(sends))
    last = (inv,)
    masks = orders(lax.axis_size("eig"))
    count = len(masks[0])
    for at in range(count + 1):
        for i in range(CHAINS):
            if at == count:
                sends[i] = add(totals[i], gots[i], last, True)
            else:
                totals[i], sends[i] = add(totals[i], gots[i], last)
                gots[i] = swap(sends[i], "eig", masks[i][at])
            last = (sends[i],)

    blocks = [sends]
    for bit in bits(groups):
        blocks = blocks + [[swap(piece, "groups", bit) for piece in block] for block in blocks]
    places = [(m, i) for m in range(groups) for i in range(CHAINS)]
    batches = [places[:CHAINS]] + [[place] for place in places[CHAINS:]]
    total = None
    for batch in batches:
        pieces = [blocks[m][i] for m, i in batch]
        total = share(batch, pieces, responses, total, inv if batch is batches[-1] else None)
    return weights(basis, total, swap(total, "eig", 1))


def solution(mesh):
    in_specs = (
        P(None, "eig"),
        P(None, "groups"),
        P("eig", None),
        P(),
        P("groups"),
        P("groups"),
        P(),
    )
    out_specs = P("eig", "groups")
    return jax.shard_map(body, mesh=mesh, in_specs=in_specs, out_specs=out_specs, check_vma=False)
```

```python
import functools

import jax
import jax.numpy as jnp
from jax import lax
from jax.experimental import pallas as pl
from jax.experimental.pallas import tpu as pltpu
from jax.sharding import PartitionSpec as P

F32 = jnp.float32
BF16 = jnp.bfloat16
MIB = 1 << 20
CHAINS = 2
EIG_FLIP = 14
GROUP_FLIP = 1
ANY = pl.BlockSpec(memory_space=pl.ANY)
HBM = pl.BlockSpec(memory_space=pltpu.HBM)
VMEM = pl.BlockSpec(memory_space=pltpu.VMEM)
SMEM = pl.BlockSpec(memory_space=pltpu.SMEM)


def params(mib):
    return pltpu.CompilerParams(vmem_limit_bytes=mib * MIB)


def cost(flops, moved):
    return pl.CostEstimate(flops=flops, bytes_accessed=moved, transcendentals=0)


def in_hbm(value):
    return pltpu.with_memory_space_constraint(value, pltpu.HBM)


def parity(value, mask):
    total = 0
    while mask:
        low = mask & -mask
        total = total + (value // low) % 2
        mask ^= low
    return total % 2


def half_index():
    return (parity(lax.axis_index("eig"), EIG_FLIP | 1) + parity(lax.axis_index("groups"), GROUP_FLIP)) % 2


def split_halves(total, kept_ref, sent_ref):
    half = kept_ref.shape[1]
    low, high = total[:, :half], total[:, half:]
    first = half_index() == 0
    kept_ref[...] = jnp.where(first, low, high)
    sent_ref[...] = jnp.where(first, high, low).astype(BF16)


def gram_first_kernel(f_hbm, b_hbm, kept_ref, sent_ref, rest_ref, b_ref, f_ref, f_sem, b_sem, rest_sem):
    rows, feats = f_ref.shape
    parts = f_sem.shape[0]
    chunk = feats // parts
    more = rest_ref.shape[0]
    start = pl.multiple_of(lax.axis_index("groups") * (rows + more), rows)
    after = pl.multiple_of(start + rows, rows)
    copies = []
    for i in range(parts):
        cols = pl.ds(i * chunk, chunk)
        b_copy = pltpu.make_async_copy(b_hbm.at[cols], b_ref.at[cols], b_sem.at[i])
        f_copy = pltpu.make_async_copy(f_hbm.at[pl.ds(start, rows), cols], f_ref.at[:, cols], f_sem.at[i])
        b_copy.start()
        f_copy.start()
        copies.append((b_copy, f_copy))
    rest_copy = pltpu.make_async_copy(f_hbm.at[pl.ds(after, more)], rest_ref, rest_sem)
    rest_copy.start()
    total = None
    for i, (b_copy, f_copy) in enumerate(copies):
        cols = pl.ds(i * chunk, chunk)
        b_copy.wait()
        f_copy.wait()
        term = jnp.dot(f_ref[:, cols], b_ref[cols, :], preferred_element_type=F32)
        total = term if total is None else total + term
    split_halves(total, kept_ref, sent_ref)
    rest_copy.wait()


def gram_rest_kernel(f_ref, b_ref, *refs):
    kept_ref, sent_ref = refs[-2:]
    split_halves(jnp.dot(f_ref[...], b_ref[...], preferred_element_type=F32), kept_ref, sent_ref)


def gram_first(features, basis, groups):
    times, feats = features.shape
    k = basis.shape[1]
    rows = times // groups // CHAINS
    parts = 2
    return pl.pallas_call(
        gram_first_kernel,
        in_specs=[HBM, HBM],
        out_specs=[VMEM] * 4,
        out_shape=[
            jax.ShapeDtypeStruct((rows, k // 2), F32),
            jax.ShapeDtypeStruct((rows, k // 2), BF16),
            jax.ShapeDtypeStruct((rows, feats), BF16),
            jax.ShapeDtypeStruct((feats, k), BF16),
        ],
        scratch_shapes=[
            pltpu.VMEM((rows, feats), BF16),
            pltpu.SemaphoreType.DMA((parts,)),
            pltpu.SemaphoreType.DMA((parts,)),
            pltpu.SemaphoreType.DMA,
        ],
        compiler_params=params(12),
        cost_estimate=cost(2 * rows * feats * k, 2 * (rows + k) * feats),
        name="gram_first",
    )(in_hbm(features), in_hbm(basis))


def gram_rest(rest, basis, after):
    rows, feats = rest.shape
    k = basis.shape[1]
    return pl.pallas_call(
        gram_rest_kernel,
        in_specs=[VMEM, VMEM] + [ANY] * len(after),
        out_specs=[VMEM] * 2,
        out_shape=[
            jax.ShapeDtypeStruct((rows, k // 2), F32),
            jax.ShapeDtypeStruct((rows, k // 2), BF16),
        ],
        compiler_params=params(8),
        cost_estimate=cost(2 * rows * feats * k, 2 * (rows + k) * feats),
        name="gram_rest",
    )(rest, basis, *after)


def inverse_kernel(table_ref, reg_ref, subject_ref, eig_ref, *refs):
    out_ref = refs[-1]
    subjects, grid = table_ref.shape
    k = out_ref.shape[0]
    code = subject_ref[...] * grid + reg_ref[...]
    alpha = jnp.zeros(code.shape, F32)
    for s in range(subjects):
        for g in range(grid):
            alpha = jnp.where(code == s * grid + g, table_ref[s, g], alpha)
    side = min(k, 128)
    first = half_index() == 0
    eig = jnp.where(first, eig_ref[:, :k], eig_ref[:, k:])
    shape = (side, side)
    diagonal = lax.broadcasted_iota(jnp.int32, shape, 0) == lax.broadcasted_iota(jnp.int32, shape, 1)
    for i in range(k // side):
        at = pl.ds(i * side, side)
        column = jnp.sum(jnp.where(diagonal, eig[:, i * side : (i + 1) * side], 0.0), axis=1, keepdims=True)
        out_ref[at, :] = 1.0 / (column + alpha)


def inverse(alpha_table, reg_index, subject, eigenvalues, after):
    vox = reg_index.shape[0]
    k = eigenvalues.shape[0] // 2
    return pl.pallas_call(
        inverse_kernel,
        in_specs=[SMEM, VMEM, VMEM, VMEM] + [ANY] * len(after),
        out_specs=VMEM,
        out_shape=jax.ShapeDtypeStruct((k, vox), F32),
        compiler_params=params(8),
        cost_estimate=cost(8 * k * vox, 2 * k * vox),
        name="inverse",
    )(alpha_table, reg_index[None, :], subject[None, :], eigenvalues[None, :], *after)


def add_kernel(total_ref, got_ref, *refs):
    out_ref, send_ref = refs[-2:]
    total = total_ref[...] + got_ref[...].astype(F32)
    out_ref[...] = total
    send_ref[...] = total.astype(BF16)


def add_last_kernel(total_ref, got_ref, *refs):
    refs[-1][...] = (total_ref[...] + got_ref[...].astype(F32)).astype(BF16)


def add(total, got, after, last=False):
    shape = total.shape
    both = [jax.ShapeDtypeStruct(shape, F32), jax.ShapeDtypeStruct(shape, BF16)]
    return pl.pallas_call(
        add_last_kernel if last else add_kernel,
        in_specs=[VMEM, VMEM] + [ANY] * len(after),
        out_specs=VMEM if last else [VMEM, VMEM],
        out_shape=both[1] if last else both,
        compiler_params=params(4),
        cost_estimate=cost(total.size, 12 * total.size),
        name="add",
    )(total, got, *after)


def share_kernel(places, has_sum, finish, *refs):
    n = len(places)
    r_ref, out_ref = refs[n], refs[-1]
    rest = list(refs[n + 1 : -1])
    group = lax.axis_index("groups")
    total = rest.pop(0)[...] if has_sum else None
    for (m, at), piece in zip(places, refs):
        rows = piece.shape[0]
        start = pl.multiple_of(((group ^ m) * CHAINS + at) * rows, rows)
        term = lax.dot_general(
            piece[...], r_ref[pl.ds(start, rows), :], (((0,), (0,)), ((), ())), preferred_element_type=F32
        )
        total = term if total is None else total + term
    if finish:
        total = total * rest.pop(0)[...]
    out_ref[...] = total.astype(out_ref.dtype)


def share(places, pieces, responses, before=None, inv=None):
    rows, k = pieces[0].shape
    vox = responses.shape[1]
    extra = [value for value in (before, inv) if value is not None]
    return pl.pallas_call(
        functools.partial(share_kernel, places, before is not None, inv is not None),
        in_specs=[VMEM] * (len(pieces) + 1 + len(extra)),
        out_specs=VMEM,
        out_shape=jax.ShapeDtypeStruct((k, vox), F32 if inv is None else BF16),
        compiler_params=params(8),
        cost_estimate=cost(2 * len(places) * rows * k * vox, 2 * rows * vox),
        name="share",
    )(*pieces, responses, *extra)


def weights_kernel(b_ref, own_ref, got_ref, out_hbm, s_ref, out_ref, sems):
    parts = sems.shape[0]
    half = own_ref.shape[0]
    first = half_index() == 0
    own, got = own_ref[...], got_ref[...]
    s_ref[:half, :] = jnp.where(first, own, got)
    s_ref[half:, :] = jnp.where(first, got, own)
    chunk = b_ref.shape[0] // parts
    copies = []
    for i in range(parts):
        rows = pl.ds(i * chunk, chunk)
        out_ref[rows, :] = jnp.dot(b_ref[rows, :], s_ref[...], preferred_element_type=F32).astype(BF16)
        copy = pltpu.make_async_copy(out_ref.at[rows], out_hbm.at[rows], sems.at[i])
        copy.start()
        copies.append(copy)
    for copy in copies:
        copy.wait()


def weights(basis, own, got):
    feats, k = basis.shape
    half, vox = own.shape
    parts = 8
    return pl.pallas_call(
        weights_kernel,
        in_specs=[VMEM, VMEM, VMEM],
        out_specs=HBM,
        out_shape=jax.ShapeDtypeStruct((feats, vox), BF16),
        scratch_shapes=[
            pltpu.VMEM((k, vox), BF16),
            pltpu.VMEM((feats, vox), BF16),
            pltpu.SemaphoreType.DMA((parts,)),
        ],
        compiler_params=params(16),
        cost_estimate=cost(2 * feats * k * vox, 2 * feats * vox),
        name="weights",
    )(basis, own, got)


def swap(value, group_mask, eig_mask):
    groups, size = lax.axis_size("groups"), lax.axis_size("eig")
    eig_mask ^= (parity(eig_mask & ~1, EIG_FLIP) + parity(group_mask, GROUP_FLIP)) % 2
    pairs = [
        (g * size + e, (g ^ group_mask) * size + (e ^ eig_mask)) for g in range(groups) for e in range(size)
    ]
    return lax.ppermute(value, ("groups", "eig"), pairs)


def bits(size):
    out = []
    while (1 << len(out)) < size:
        out.append(1 << len(out))
    return out


def orders(size):
    steps = bits(size)[1:]
    return [steps, steps[1:] + steps[:1]]


def body(features, responses, basis, eigenvalues, reg_index, subject, alpha_table):
    groups = lax.axis_size("groups")
    total, send, rest, panel = gram_first(features, basis, groups)
    totals, gots = [total], [swap(send, 0, 1)]
    total, send = gram_rest(rest, panel, (send,))
    totals.append(total)
    gots.append(swap(send, 0, 1))
    sends = [None] * CHAINS
    last = (send,)
    masks = orders(lax.axis_size("eig"))
    count = len(masks[0])
    for at in range(count + 1):
        if at == count:
            inv = inverse(alpha_table, reg_index, subject, eigenvalues, last)
            last = (inv,)
        for i in range(CHAINS):
            if at == count:
                sends[i] = add(totals[i], gots[i], last, True)
            else:
                totals[i], sends[i] = add(totals[i], gots[i], last)
                gots[i] = swap(sends[i], 0, masks[i][at])
            last = (sends[i],)

    blocks = [sends]
    for bit in bits(groups):
        blocks = blocks + [[swap(piece, bit, 0) for piece in block] for block in blocks]
    places = [(m, i) for m in range(groups) for i in range(CHAINS)]
    batches = [places[:CHAINS]] + [[place] for place in places[CHAINS:]]
    total = None
    for batch in batches:
        pieces = [blocks[m][i] for m, i in batch]
        total = share(batch, pieces, responses, total, inv if batch is batches[-1] else None)
    return weights(panel, total, swap(total, 0, 1))


def solution(mesh):
    in_specs = (
        P(None, "eig"),
        P(None, "groups"),
        P("eig", None),
        P(),
        P("groups"),
        P("groups"),
        P(),
    )
    out_specs = P("eig", "groups")
    return jax.shard_map(body, mesh=mesh, in_specs=in_specs, out_specs=out_specs, check_vma=False)
```

```python
import functools

import jax
import jax.numpy as jnp
from jax import lax
from jax.experimental import pallas as pl
from jax.experimental.pallas import tpu as pltpu
from jax.sharding import PartitionSpec as P

F32 = jnp.float32
BF16 = jnp.bfloat16
MIB = 1 << 20
CHAINS = 2
EIG_FLIP = 14
GROUP_FLIP = 1
FIRST = 8
ANY = pl.BlockSpec(memory_space=pl.ANY)
HBM = pl.BlockSpec(memory_space=pltpu.HBM)
VMEM = pl.BlockSpec(memory_space=pltpu.VMEM)
SMEM = pl.BlockSpec(memory_space=pltpu.SMEM)


def params(mib):
    return pltpu.CompilerParams(vmem_limit_bytes=mib * MIB)


def cost(flops, moved):
    return pl.CostEstimate(flops=flops, bytes_accessed=moved, transcendentals=0)


def in_hbm(value):
    return pltpu.with_memory_space_constraint(value, pltpu.HBM)


def parity(value, mask):
    total = 0
    while mask:
        low = mask & -mask
        total = total + (value // low) % 2
        mask ^= low
    return total % 2


def half_of(group, eig):
    return (parity(eig, EIG_FLIP | 1) + parity(group, GROUP_FLIP)) % 2


def half_index():
    return half_of(lax.axis_index("groups"), lax.axis_index("eig"))


def chain_rows(times):
    first = times * FIRST // 16
    return first, times - first


def split_halves(total, kept_ref, sent_ref):
    half = kept_ref.shape[1]
    low, high = total[:, :half], total[:, half:]
    first = half_index() == 0
    kept_ref[...] = jnp.where(first, low, high)
    sent_ref[...] = jnp.where(first, high, low).astype(BF16)


def gram_first_kernel(f_hbm, b_hbm, kept_ref, sent_ref, rest_ref, b_ref, f_ref, f_sem, b_sem, rest_sem):
    rows, feats = f_ref.shape
    parts = f_sem.shape[0]
    chunk = feats // parts
    more = rest_ref.shape[0]
    start = pl.multiple_of(lax.axis_index("groups") * (rows + more), 16)
    after = pl.multiple_of(start + rows, 16)
    copies = []
    for i in range(parts):
        cols = pl.ds(i * chunk, chunk)
        b_copy = pltpu.make_async_copy(b_hbm.at[cols], b_ref.at[cols], b_sem.at[i])
        f_copy = pltpu.make_async_copy(f_hbm.at[pl.ds(start, rows), cols], f_ref.at[:, cols], f_sem.at[i])
        b_copy.start()
        f_copy.start()
        copies.append((b_copy, f_copy))
    rest_copy = pltpu.make_async_copy(f_hbm.at[pl.ds(after, more)], rest_ref, rest_sem)
    rest_copy.start()
    total = None
    for i, (b_copy, f_copy) in enumerate(copies):
        cols = pl.ds(i * chunk, chunk)
        b_copy.wait()
        f_copy.wait()
        term = jnp.dot(f_ref[:, cols], b_ref[cols, :], preferred_element_type=F32)
        total = term if total is None else total + term
    split_halves(total, kept_ref, sent_ref)
    rest_copy.wait()


def gram_rest_kernel(f_ref, b_ref, *refs):
    kept_ref, sent_ref = refs[-2:]
    split_halves(jnp.dot(f_ref[...], b_ref[...], preferred_element_type=F32), kept_ref, sent_ref)


def gram_first(features, basis, groups):
    times, feats = features.shape
    k = basis.shape[1]
    rows, more = chain_rows(times // groups)
    parts = 2
    return pl.pallas_call(
        gram_first_kernel,
        in_specs=[HBM, HBM],
        out_specs=[VMEM] * 4,
        out_shape=[
            jax.ShapeDtypeStruct((rows, k // 2), F32),
            jax.ShapeDtypeStruct((rows, k // 2), BF16),
            jax.ShapeDtypeStruct((more, feats), BF16),
            jax.ShapeDtypeStruct((feats, k), BF16),
        ],
        scratch_shapes=[
            pltpu.VMEM((rows, feats), BF16),
            pltpu.SemaphoreType.DMA((parts,)),
            pltpu.SemaphoreType.DMA((parts,)),
            pltpu.SemaphoreType.DMA,
        ],
        compiler_params=params(12),
        cost_estimate=cost(2 * rows * feats * k, 2 * (rows + k) * feats),
        name="gram_first",
    )(in_hbm(features), in_hbm(basis))


def gram_rest(rest, basis, after):
    rows, feats = rest.shape
    k = basis.shape[1]
    return pl.pallas_call(
        gram_rest_kernel,
        in_specs=[VMEM, VMEM] + [ANY] * len(after),
        out_specs=[VMEM] * 2,
        out_shape=[
            jax.ShapeDtypeStruct((rows, k // 2), F32),
            jax.ShapeDtypeStruct((rows, k // 2), BF16),
        ],
        compiler_params=params(8),
        cost_estimate=cost(2 * rows * feats * k, 2 * (rows + k) * feats),
        name="gram_rest",
    )(rest, basis, *after)


def inverse_kernel(table_ref, reg_ref, subject_ref, eig_ref, *refs):
    out_ref = refs[-1]
    subjects, grid = table_ref.shape
    k = out_ref.shape[0]
    code = subject_ref[...] * grid + reg_ref[...]
    alpha = jnp.zeros(code.shape, F32)
    for s in range(subjects):
        for g in range(grid):
            alpha = jnp.where(code == s * grid + g, table_ref[s, g], alpha)
    alpha = alpha.reshape(1, alpha.size)
    side = min(k, 128)
    first = half_index() == 0
    eig = jnp.where(first, eig_ref[:, :k], eig_ref[:, k:])
    shape = (side, side)
    diagonal = lax.broadcasted_iota(jnp.int32, shape, 0) == lax.broadcasted_iota(jnp.int32, shape, 1)
    for i in range(k // side):
        at = pl.ds(i * side, side)
        column = jnp.sum(jnp.where(diagonal, eig[:, i * side : (i + 1) * side], 0.0), axis=1, keepdims=True)
        out_ref[at, :] = 1.0 / (column + alpha)


def inverse(alpha_table, reg_index, subject, eigenvalues, after):
    vox = reg_index.shape[0]
    k = eigenvalues.shape[0] // 2
    return pl.pallas_call(
        inverse_kernel,
        in_specs=[SMEM, VMEM, VMEM, VMEM] + [ANY] * len(after),
        out_specs=VMEM,
        out_shape=jax.ShapeDtypeStruct((k, vox), F32),
        compiler_params=params(8),
        cost_estimate=cost(8 * k * vox, 2 * k * vox),
        name="inverse",
    )(alpha_table, reg_index.reshape(-1, 128), subject.reshape(-1, 128), eigenvalues[None, :], *after)


def add_kernel(total_ref, got_ref, *refs):
    out_ref, send_ref = refs[-2:]
    total = total_ref[...] + got_ref[...].astype(F32)
    out_ref[...] = total
    send_ref[...] = total.astype(BF16)


def add_last_kernel(total_ref, got_ref, *refs):
    refs[-1][...] = (total_ref[...] + got_ref[...].astype(F32)).astype(BF16)


def add(total, got, after, last=False):
    shape = total.shape
    both = [jax.ShapeDtypeStruct(shape, F32), jax.ShapeDtypeStruct(shape, BF16)]
    return pl.pallas_call(
        add_last_kernel if last else add_kernel,
        in_specs=[VMEM, VMEM] + [ANY] * len(after),
        out_specs=VMEM if last else [VMEM, VMEM],
        out_shape=both[1] if last else both,
        compiler_params=params(4),
        cost_estimate=cost(total.size, 12 * total.size),
        name="add",
    )(total, got, *after)


def share_kernel(places, has_sum, finish, *refs):
    n = len(places)
    r_ref, out_ref = refs[n], refs[-1]
    rest = list(refs[n + 1 : -1])
    group = lax.axis_index("groups")
    times = r_ref.shape[0] // lax.axis_size("groups")
    total = rest.pop(0)[...] if has_sum else None
    for (m, at), piece in zip(places, refs):
        rows = piece.shape[0]
        start = pl.multiple_of((group ^ m) * times + at, 16)
        term = lax.dot_general(
            piece[...], r_ref[pl.ds(start, rows), :], (((0,), (0,)), ((), ())), preferred_element_type=F32
        )
        total = term if total is None else total + term
    if finish:
        total = total * rest.pop(0)[...]
    out_ref[...] = total.astype(out_ref.dtype)


def share(places, pieces, responses, before=None, inv=None):
    rows, k = pieces[0].shape
    vox = responses.shape[1]
    extra = [value for value in (before, inv) if value is not None]
    return pl.pallas_call(
        functools.partial(share_kernel, places, before is not None, inv is not None),
        in_specs=[VMEM] * (len(pieces) + 1 + len(extra)),
        out_specs=VMEM,
        out_shape=jax.ShapeDtypeStruct((k, vox), F32 if inv is None else BF16),
        compiler_params=params(8),
        cost_estimate=cost(2 * len(places) * rows * k * vox, 2 * rows * vox),
        name="share",
    )(*pieces, responses, *extra)


def weights_kernel(b_ref, own_ref, got_ref, out_hbm, s_ref, out_ref, sems):
    parts = sems.shape[0]
    half = own_ref.shape[0]
    first = half_index() == 0
    own, got = own_ref[...], got_ref[...]
    s_ref[:half, :] = jnp.where(first, own, got)
    s_ref[half:, :] = jnp.where(first, got, own)
    chunk = b_ref.shape[0] // parts
    copies = []
    for i in range(parts):
        rows = pl.ds(i * chunk, chunk)
        out_ref[rows, :] = jnp.dot(b_ref[rows, :], s_ref[...], preferred_element_type=F32).astype(BF16)
        copy = pltpu.make_async_copy(out_ref.at[rows], out_hbm.at[rows], sems.at[i])
        copy.start()
        copies.append(copy)
    for copy in copies:
        copy.wait()


def weights(basis, own, got):
    feats, k = basis.shape
    half, vox = own.shape
    parts = 8
    return pl.pallas_call(
        weights_kernel,
        in_specs=[VMEM, VMEM, VMEM],
        out_specs=HBM,
        out_shape=jax.ShapeDtypeStruct((feats, vox), BF16),
        scratch_shapes=[
            pltpu.VMEM((k, vox), BF16),
            pltpu.VMEM((feats, vox), BF16),
            pltpu.SemaphoreType.DMA((parts,)),
        ],
        compiler_params=params(16),
        cost_estimate=cost(2 * feats * k * vox, 2 * feats * vox),
        name="weights",
    )(basis, own, got)


def swap(value, group_mask, eig_masks):
    groups, size = lax.axis_size("groups"), lax.axis_size("eig")
    pairs = []
    for g in range(groups):
        for e in range(size):
            mask = eig_masks[half_of(g, e)]
            mask ^= (parity(mask & ~1, EIG_FLIP) + parity(group_mask, GROUP_FLIP)) % 2
            pairs.append((g * size + e, (g ^ group_mask) * size + (e ^ mask)))
    return lax.ppermute(value, ("groups", "eig"), pairs)


def bits(size):
    out = []
    while (1 << len(out)) < size:
        out.append(1 << len(out))
    return out


def orders(size):
    steps = bits(size)[1:]
    turn = [steps[i:] + steps[:i] for i in range(len(steps))]
    return [[turn[0], turn[-1]], [turn[1 % len(steps)], turn[-1]]]


def body(features, responses, basis, eigenvalues, reg_index, subject, alpha_table):
    groups = lax.axis_size("groups")
    total, send, rest, panel = gram_first(features, basis, groups)
    totals, gots = [total], [swap(send, 0, (1, 1))]
    total, send = gram_rest(rest, panel, (send,))
    totals.append(total)
    gots.append(swap(send, 0, (1, 1)))
    sends = [None] * CHAINS
    last = (send,)
    masks = orders(lax.axis_size("eig"))
    count = len(masks[0][0])
    for at in range(count + 1):
        for i in range(CHAINS):
            if at == count:
                sends[i] = add(totals[i], gots[i], last, True)
            else:
                totals[i], sends[i] = add(totals[i], gots[i], last)
                gots[i] = swap(sends[i], 0, [masks[i][half][at] for half in range(2)])
            last = (sends[i],)

    inv = inverse(alpha_table, reg_index, subject, eigenvalues, last)
    blocks = [sends]
    for bit in bits(groups):
        blocks = blocks + [[swap(piece, bit, (0, 0)) for piece in block] for block in blocks]
    places = [(m, i) for m in range(groups) for i in range(CHAINS)]
    offsets = (0, sends[0].shape[0])
    batches = [places[:CHAINS]] + [[place] for place in places[CHAINS:]]
    total = None
    for batch in batches:
        pieces = [blocks[m][i] for m, i in batch]
        total = share([(m, offsets[i]) for m, i in batch], pieces, responses, total, inv if batch is batches[-1] else None)
    return weights(panel, total, swap(total, 0, (1, 1)))


def solution(mesh):
    in_specs = (
        P(None, "eig"),
        P(None, "groups"),
        P("eig", None),
        P(),
        P("groups"),
        P("groups"),
        P(),
    )
    out_specs = P("eig", "groups")
    return jax.shard_map(body, mesh=mesh, in_specs=in_specs, out_specs=out_specs, check_vma=False)
```

```python
import functools

import jax
import jax.numpy as jnp
from jax import lax
from jax.experimental import pallas as pl
from jax.experimental.pallas import tpu as pltpu
from jax.sharding import PartitionSpec as P

F32 = jnp.float32
BF16 = jnp.bfloat16
MIB = 1 << 20
CHAINS = 2
EIG_FLIP = 10
GROUP_FLIP = 1
FIRST = 8
ANY = pl.BlockSpec(memory_space=pl.ANY)
HBM = pl.BlockSpec(memory_space=pltpu.HBM)
VMEM = pl.BlockSpec(memory_space=pltpu.VMEM)


def params(mib):
    return pltpu.CompilerParams(vmem_limit_bytes=mib * MIB)


def cost(flops, moved):
    return pl.CostEstimate(flops=flops, bytes_accessed=moved, transcendentals=0)


def in_hbm(value):
    return pltpu.with_memory_space_constraint(value, pltpu.HBM)


def parity(value, mask):
    total = 0
    while mask:
        low = mask & -mask
        total = total + (value // low) % 2
        mask ^= low
    return total % 2


def half_of(group, eig):
    return (parity(eig, EIG_FLIP | 1) + parity(group, GROUP_FLIP)) % 2


def half_index():
    return half_of(lax.axis_index("groups"), lax.axis_index("eig"))


def chain_rows(times):
    first = times * FIRST // 16
    return first, times - first


def split_halves(total, kept_ref, sent_ref):
    half = kept_ref.shape[1]
    low, high = total[:, :half], total[:, half:]
    first = half_index() == 0
    kept_ref[...] = jnp.where(first, low, high)
    sent_ref[...] = jnp.where(first, high, low).astype(BF16)


def gram_first_kernel(f_hbm, b_hbm, kept_ref, sent_ref, rest_ref, b_ref, f_ref, f_sem, b_sem, rest_sem):
    rows, feats = f_ref.shape
    parts = f_sem.shape[0]
    chunk = feats // parts
    more = rest_ref.shape[0]
    start = pl.multiple_of(lax.axis_index("groups") * (rows + more), 16)
    after = pl.multiple_of(start + rows, 16)
    copies = []
    for i in range(parts):
        cols = pl.ds(i * chunk, chunk)
        b_copy = pltpu.make_async_copy(b_hbm.at[cols], b_ref.at[cols], b_sem.at[i])
        f_copy = pltpu.make_async_copy(f_hbm.at[pl.ds(start, rows), cols], f_ref.at[:, cols], f_sem.at[i])
        b_copy.start()
        f_copy.start()
        copies.append((b_copy, f_copy))
    rest_copy = pltpu.make_async_copy(f_hbm.at[pl.ds(after, more)], rest_ref, rest_sem)
    rest_copy.start()
    total = None
    for i, (b_copy, f_copy) in enumerate(copies):
        cols = pl.ds(i * chunk, chunk)
        b_copy.wait()
        f_copy.wait()
        term = jnp.dot(f_ref[:, cols], b_ref[cols, :], preferred_element_type=F32)
        total = term if total is None else total + term
    split_halves(total, kept_ref, sent_ref)
    rest_copy.wait()


def gram_rest_kernel(f_ref, b_ref, *refs):
    kept_ref, sent_ref = refs[-2:]
    split_halves(jnp.dot(f_ref[...], b_ref[...], preferred_element_type=F32), kept_ref, sent_ref)


def gram_first(features, basis, groups):
    times, feats = features.shape
    k = basis.shape[1]
    rows, more = chain_rows(times // groups)
    parts = 2
    return pl.pallas_call(
        gram_first_kernel,
        in_specs=[HBM, HBM],
        out_specs=[VMEM] * 4,
        out_shape=[
            jax.ShapeDtypeStruct((rows, k // 2), F32),
            jax.ShapeDtypeStruct((rows, k // 2), BF16),
            jax.ShapeDtypeStruct((more, feats), BF16),
            jax.ShapeDtypeStruct((feats, k), BF16),
        ],
        scratch_shapes=[
            pltpu.VMEM((rows, feats), BF16),
            pltpu.SemaphoreType.DMA((parts,)),
            pltpu.SemaphoreType.DMA((parts,)),
            pltpu.SemaphoreType.DMA,
        ],
        compiler_params=params(12),
        cost_estimate=cost(2 * rows * feats * k, 2 * (rows + k) * feats),
        name="gram_first",
    )(in_hbm(features), in_hbm(basis))


def gram_rest(rest, basis, after):
    rows, feats = rest.shape
    k = basis.shape[1]
    return pl.pallas_call(
        gram_rest_kernel,
        in_specs=[VMEM, VMEM] + [ANY] * len(after),
        out_specs=[VMEM] * 2,
        out_shape=[
            jax.ShapeDtypeStruct((rows, k // 2), F32),
            jax.ShapeDtypeStruct((rows, k // 2), BF16),
        ],
        compiler_params=params(8),
        cost_estimate=cost(2 * rows * feats * k, 2 * (rows + k) * feats),
        name="gram_rest",
    )(rest, basis, *after)


def inverse_kernel(table_ref, reg_ref, subject_ref, eig_ref, *refs):
    out_ref = refs[-1]
    subjects, grid = table_ref.shape
    k, vox = out_ref.shape
    picked = lax.broadcasted_iota(jnp.int32, (grid, vox), 0) == reg_ref[...]
    rows = jnp.dot(
        table_ref[...], picked.astype(F32), precision=lax.Precision.HIGHEST, preferred_element_type=F32
    )
    mine = lax.broadcasted_iota(jnp.int32, (subjects, vox), 0) == subject_ref[...]
    alpha = jnp.sum(jnp.where(mine, rows, 0.0), axis=0, keepdims=True)
    side = min(k, 128)
    shape = (side, side)
    diagonal = lax.broadcasted_iota(jnp.int32, shape, 0) == lax.broadcasted_iota(jnp.int32, shape, 1)
    for i in range(k // side):
        at = pl.ds(i * side, side)
        column = jnp.sum(jnp.where(diagonal, eig_ref[:, pl.ds(i * side, side)], 0.0), axis=1, keepdims=True)
        out_ref[at, :] = 1.0 / (column + alpha)


def inverse(alpha_table, reg_index, subject, eigenvalues, after):
    vox = reg_index.shape[0]
    k = eigenvalues.shape[0]
    return pl.pallas_call(
        inverse_kernel,
        in_specs=[VMEM, VMEM, VMEM, VMEM] + [ANY] * len(after),
        out_specs=VMEM,
        out_shape=jax.ShapeDtypeStruct((k, vox), F32),
        compiler_params=params(8),
        cost_estimate=cost(8 * k * vox, 2 * k * vox),
        name="inverse",
    )(alpha_table, reg_index[None, :], subject[None, :], eigenvalues[None, :], *after)


def add_kernel(total_ref, got_ref, *refs):
    out_ref, send_ref = refs[-2:]
    total = total_ref[...] + got_ref[...].astype(F32)
    out_ref[...] = total
    send_ref[...] = total.astype(BF16)


def add_last_kernel(total_ref, got_ref, *refs):
    refs[-1][...] = (total_ref[...] + got_ref[...].astype(F32)).astype(BF16)


def add(total, got, after, last=False):
    shape = total.shape
    both = [jax.ShapeDtypeStruct(shape, F32), jax.ShapeDtypeStruct(shape, BF16)]
    return pl.pallas_call(
        add_last_kernel if last else add_kernel,
        in_specs=[VMEM, VMEM] + [ANY] * len(after),
        out_specs=VMEM if last else [VMEM, VMEM],
        out_shape=both[1] if last else both,
        compiler_params=params(4),
        cost_estimate=cost(4 * 10**9, 12 * total.size),
        name="add",
    )(total, got, *after)


def share_kernel(places, has_sum, finish, *refs):
    n = 2 * len(places)
    r_ref, out_ref = refs[n], refs[-1]
    rest = list(refs[n + 1 : -1])
    group = lax.axis_index("groups")
    first = half_index() == 0
    times = r_ref.shape[0] // lax.axis_size("groups")
    total = rest.pop(0)[...] if has_sum else None
    for i, (m, at) in enumerate(places):
        own, got = refs[2 * i][...], refs[2 * i + 1][...]
        piece = jnp.concatenate([jnp.where(first, own, got), jnp.where(first, got, own)], axis=1)
        start = pl.multiple_of((group ^ m) * times + at, 16)
        term = lax.dot_general(
            piece,
            r_ref[pl.ds(start, piece.shape[0]), :],
            (((0,), (0,)), ((), ())),
            preferred_element_type=F32,
        )
        total = term if total is None else total + term
    if finish:
        total = total * rest.pop(0)[...]
    out_ref[...] = total.astype(out_ref.dtype)


def share(places, pieces, responses, before=None, inv=None):
    rows, k = pieces[0].shape[0], 2 * pieces[0].shape[1]
    vox = responses.shape[1]
    extra = [value for value in (before, inv) if value is not None]
    return pl.pallas_call(
        functools.partial(share_kernel, places, before is not None, inv is not None),
        in_specs=[VMEM] * (len(pieces) + 1 + len(extra)),
        out_specs=VMEM,
        out_shape=jax.ShapeDtypeStruct((k, vox), F32 if inv is None else BF16),
        compiler_params=params(8),
        cost_estimate=cost(2 * len(places) * rows * k * vox, 2 * rows * vox),
        name="share",
    )(*pieces, responses, *extra)


def weights_kernel(b_ref, s_ref, out_hbm, out_ref, sems):
    parts = sems.shape[0]
    chunk = b_ref.shape[0] // parts
    copies = []
    for i in range(parts):
        rows = pl.ds(i * chunk, chunk)
        out_ref[rows, :] = jnp.dot(b_ref[rows, :], s_ref[...], preferred_element_type=F32).astype(BF16)
        copy = pltpu.make_async_copy(out_ref.at[rows], out_hbm.at[rows], sems.at[i])
        copy.start()
        copies.append(copy)
    for copy in copies:
        copy.wait()


def weights(basis, scaled):
    feats, k = basis.shape
    vox = scaled.shape[1]
    parts = 8
    return pl.pallas_call(
        weights_kernel,
        in_specs=[VMEM, VMEM],
        out_specs=HBM,
        out_shape=jax.ShapeDtypeStruct((feats, vox), BF16),
        scratch_shapes=[pltpu.VMEM((feats, vox), BF16), pltpu.SemaphoreType.DMA((parts,))],
        compiler_params=params(16),
        cost_estimate=cost(2 * feats * k * vox, 2 * feats * vox),
        name="weights",
    )(basis, scaled)


def swap(value, group_mask, eig_masks):
    groups, size = lax.axis_size("groups"), lax.axis_size("eig")
    pairs = []
    for g in range(groups):
        for e in range(size):
            mask = eig_masks[half_of(g, e)]
            mask ^= (parity(mask & ~1, EIG_FLIP) + parity(group_mask, GROUP_FLIP)) % 2
            pairs.append((g * size + e, (g ^ group_mask) * size + (e ^ mask)))
    return lax.ppermute(value, ("groups", "eig"), pairs)


def bits(size):
    out = []
    while (1 << len(out)) < size:
        out.append(1 << len(out))
    return out


def orders(size):
    steps = bits(size)[1:]
    turn = [steps[i:] + steps[:i] for i in range(len(steps))]
    return [[turn[0], turn[-1]], [turn[1 % len(steps)], turn[-1]]]


def body(features, responses, basis, eigenvalues, reg_index, subject, alpha_table):
    groups = lax.axis_size("groups")
    total, send, rest, panel = gram_first(features, basis, groups)
    totals, gots = [total], [swap(send, 0, (1, 1))]
    total, send = gram_rest(rest, panel, (send,))
    totals.append(total)
    gots.append(swap(send, 0, (1, 1)))
    sends = [None] * CHAINS
    last = (send,)
    masks = orders(lax.axis_size("eig"))
    count = len(masks[0][0])
    for at in range(count + 1):
        if at == count:
            inv = inverse(alpha_table, reg_index, subject, eigenvalues, last)
            last = (inv,)
        for i in range(CHAINS):
            if at == count:
                sends[i] = add(totals[i], gots[i], last, True)
            else:
                totals[i], sends[i] = add(totals[i], gots[i], last)
                gots[i] = swap(sends[i], 0, [masks[i][half][at] for half in range(2)])
            last = (sends[i],)

    blocks = [sends]
    for bit in bits(groups):
        blocks = blocks + [[swap(piece, bit, (0, 0)) for piece in block] for block in blocks]
    offsets = (0, sends[0].shape[0])
    places = [(m, i) for m in range(groups) for i in range(CHAINS)]
    batches = [places[:CHAINS]] + [[place] for place in places[CHAINS:]]
    total = None
    for batch in batches:
        pieces = []
        for m, i in batch:
            pieces += [blocks[m][i], swap(blocks[m][i], 0, (1, 1))]
        total = share([(m, offsets[i]) for m, i in batch], pieces, responses, total, inv if batch is batches[-1] else None)
    return weights(panel, total)


def solution(mesh):
    in_specs = (
        P(None, "eig"),
        P(None, "groups"),
        P("eig", None),
        P(),
        P("groups"),
        P("groups"),
        P(),
    )
    out_specs = P("eig", "groups")
    return jax.shard_map(body, mesh=mesh, in_specs=in_specs, out_specs=out_specs, check_vma=False)
```

```python
import functools

import jax
import jax.numpy as jnp
from jax import lax
from jax.experimental import pallas as pl
from jax.experimental.pallas import tpu as pltpu
from jax.sharding import PartitionSpec as P

F32 = jnp.float32
BF16 = jnp.bfloat16
MIB = 1 << 20
CHAINS = 2
BLOCKS = (1, 2, 2, 2, 2, 2, 2, 2, 1)
EIG_FLIP = 10
GROUP_FLIP = 1
FIRST = 8
ANY = pl.BlockSpec(memory_space=pl.ANY)
HBM = pl.BlockSpec(memory_space=pltpu.HBM)
VMEM = pl.BlockSpec(memory_space=pltpu.VMEM)


def params(mib):
    return pltpu.CompilerParams(vmem_limit_bytes=mib * MIB)


def cost(flops, moved):
    return pl.CostEstimate(flops=flops, bytes_accessed=moved, transcendentals=0)


def in_hbm(value):
    return pltpu.with_memory_space_constraint(value, pltpu.HBM)


def parity(value, mask):
    total = 0
    while mask:
        low = mask & -mask
        total = total + (value // low) % 2
        mask ^= low
    return total % 2


def half_of(group, eig):
    return (parity(eig, EIG_FLIP | 1) + parity(group, GROUP_FLIP)) % 2


def half_index():
    return half_of(lax.axis_index("groups"), lax.axis_index("eig"))


def chain_rows(times):
    first = times * FIRST // 16
    return first, times - first


def split_halves(total, kept_ref, sent_ref):
    half = kept_ref.shape[1]
    low, high = total[:, :half], total[:, half:]
    first = half_index() == 0
    kept_ref[...] = jnp.where(first, low, high)
    sent_ref[...] = jnp.where(first, high, low).astype(BF16)


def gram_first_kernel(f_hbm, b_hbm, kept_ref, sent_ref, rest_ref, b_ref, f_ref, f_sem, b_sem, rest_sem):
    rows, feats = f_ref.shape
    parts = f_sem.shape[0]
    chunk = feats // parts
    more = rest_ref.shape[0]
    start = pl.multiple_of(lax.axis_index("groups") * (rows + more), 16)
    after = pl.multiple_of(start + rows, 16)
    copies = []
    for i in range(parts):
        cols = pl.ds(i * chunk, chunk)
        b_copy = pltpu.make_async_copy(b_hbm.at[cols], b_ref.at[cols], b_sem.at[i])
        f_copy = pltpu.make_async_copy(f_hbm.at[pl.ds(start, rows), cols], f_ref.at[:, cols], f_sem.at[i])
        b_copy.start()
        f_copy.start()
        copies.append((b_copy, f_copy))
    rest_copy = pltpu.make_async_copy(f_hbm.at[pl.ds(after, more)], rest_ref, rest_sem)
    rest_copy.start()
    total = None
    for i, (b_copy, f_copy) in enumerate(copies):
        cols = pl.ds(i * chunk, chunk)
        b_copy.wait()
        f_copy.wait()
        term = jnp.dot(f_ref[:, cols], b_ref[cols, :], preferred_element_type=F32)
        total = term if total is None else total + term
    split_halves(total, kept_ref, sent_ref)
    rest_copy.wait()


def gram_rest_kernel(f_ref, b_ref, *refs):
    kept_ref, sent_ref = refs[-2:]
    split_halves(jnp.dot(f_ref[...], b_ref[...], preferred_element_type=F32), kept_ref, sent_ref)


def gram_first(features, basis, groups):
    times, feats = features.shape
    k = basis.shape[1]
    rows, more = chain_rows(times // groups)
    parts = 2
    return pl.pallas_call(
        gram_first_kernel,
        in_specs=[HBM, HBM],
        out_specs=[VMEM] * 4,
        out_shape=[
            jax.ShapeDtypeStruct((rows, k // 2), F32),
            jax.ShapeDtypeStruct((rows, k // 2), BF16),
            jax.ShapeDtypeStruct((more, feats), BF16),
            jax.ShapeDtypeStruct((feats, k), BF16),
        ],
        scratch_shapes=[
            pltpu.VMEM((rows, feats), BF16),
            pltpu.SemaphoreType.DMA((parts,)),
            pltpu.SemaphoreType.DMA((parts,)),
            pltpu.SemaphoreType.DMA,
        ],
        compiler_params=params(12),
        cost_estimate=cost(2 * rows * feats * k, 2 * (rows + k) * feats),
        name="gram_first",
    )(in_hbm(features), in_hbm(basis))


def gram_rest(rest, basis, after):
    rows, feats = rest.shape
    k = basis.shape[1]
    return pl.pallas_call(
        gram_rest_kernel,
        in_specs=[VMEM, VMEM] + [ANY] * len(after),
        out_specs=[VMEM] * 2,
        out_shape=[
            jax.ShapeDtypeStruct((rows, k // 2), F32),
            jax.ShapeDtypeStruct((rows, k // 2), BF16),
        ],
        compiler_params=params(8),
        cost_estimate=cost(2 * rows * feats * k, 2 * (rows + k) * feats),
        name="gram_rest",
    )(rest, basis, *after)


def inverse_kernel(table_ref, reg_ref, subject_ref, eig_ref, *refs):
    out_ref = refs[-1]
    subjects, grid = table_ref.shape
    k, vox = out_ref.shape
    picked = lax.broadcasted_iota(jnp.int32, (grid, vox), 0) == reg_ref[...]
    rows = jnp.dot(
        table_ref[...], picked.astype(F32), precision=lax.Precision.HIGHEST, preferred_element_type=F32
    )
    mine = lax.broadcasted_iota(jnp.int32, (subjects, vox), 0) == subject_ref[...]
    alpha = jnp.sum(jnp.where(mine, rows, 0.0), axis=0, keepdims=True)
    side = min(k, 128)
    shape = (side, side)
    diagonal = lax.broadcasted_iota(jnp.int32, shape, 0) == lax.broadcasted_iota(jnp.int32, shape, 1)
    for i in range(k // side):
        at = pl.ds(i * side, side)
        column = jnp.sum(jnp.where(diagonal, eig_ref[:, pl.ds(i * side, side)], 0.0), axis=1, keepdims=True)
        out_ref[at, :] = 1.0 / (column + alpha)


def inverse(alpha_table, reg_index, subject, eigenvalues, after):
    vox = reg_index.shape[0]
    k = eigenvalues.shape[0]
    return pl.pallas_call(
        inverse_kernel,
        in_specs=[VMEM, VMEM, VMEM, VMEM] + [ANY] * len(after),
        out_specs=VMEM,
        out_shape=jax.ShapeDtypeStruct((k, vox), F32),
        compiler_params=params(8),
        cost_estimate=cost(8 * k * vox, 2 * k * vox),
        name="inverse",
    )(alpha_table, reg_index[None, :], subject[None, :], eigenvalues[None, :], *after)


def add_kernel(total_ref, got_ref, *refs):
    out_ref, send_ref = refs[-2:]
    total = total_ref[...] + got_ref[...].astype(F32)
    out_ref[...] = total
    send_ref[...] = total.astype(BF16)


def add_last_kernel(total_ref, got_ref, *refs):
    refs[-1][...] = (total_ref[...] + got_ref[...].astype(F32)).astype(BF16)


def add(total, got, after, last=False):
    shape = total.shape
    both = [jax.ShapeDtypeStruct(shape, F32), jax.ShapeDtypeStruct(shape, BF16)]
    return pl.pallas_call(
        add_last_kernel if last else add_kernel,
        in_specs=[VMEM, VMEM] + [ANY] * len(after),
        out_specs=VMEM if last else [VMEM, VMEM],
        out_shape=both[1] if last else both,
        compiler_params=params(4),
        cost_estimate=cost(4 * 10**9, 12 * total.size),
        name="add",
    )(total, got, *after)


def share_kernel(places, has_sum, finish, *refs):
    n = 2 * len(places)
    r_ref, out_ref = refs[n], refs[-1]
    rest = list(refs[n + 1 : -1])
    group = lax.axis_index("groups")
    first = half_index() == 0
    times = r_ref.shape[0] // lax.axis_size("groups")
    total = rest.pop(0)[...] if has_sum else None
    for i, (m, at) in enumerate(places):
        own, got = refs[2 * i][...], refs[2 * i + 1][...]
        piece = jnp.concatenate([jnp.where(first, own, got), jnp.where(first, got, own)], axis=1)
        start = pl.multiple_of((group ^ m) * times + at, 16)
        term = lax.dot_general(
            piece,
            r_ref[pl.ds(start, piece.shape[0]), :],
            (((0,), (0,)), ((), ())),
            preferred_element_type=F32,
        )
        total = term if total is None else total + term
    if finish:
        total = total * rest.pop(0)[...]
    out_ref[...] = total.astype(out_ref.dtype)


def share(places, pieces, responses, before=None, inv=None):
    rows, k = pieces[0].shape[0], 2 * pieces[0].shape[1]
    vox = responses.shape[1]
    extra = [value for value in (before, inv) if value is not None]
    return pl.pallas_call(
        functools.partial(share_kernel, places, before is not None, inv is not None),
        in_specs=[VMEM] * (len(pieces) + 1 + len(extra)),
        out_specs=VMEM,
        out_shape=jax.ShapeDtypeStruct((k, vox), F32 if inv is None else BF16),
        compiler_params=params(8),
        cost_estimate=cost(2 * len(places) * rows * k * vox, 2 * rows * vox),
        name="share",
    )(*pieces, responses, *extra)


def weights_kernel(m, at, own_ref, got_ref, r_ref, before_ref, inverse_ref, b_ref, out_hbm, s_ref, out_ref, sems):
    group = lax.axis_index("groups")
    first = half_index() == 0
    own, got = own_ref[...], got_ref[...]
    piece = jnp.concatenate([jnp.where(first, own, got), jnp.where(first, got, own)], axis=1)
    times = r_ref.shape[0] // lax.axis_size("groups")
    start = pl.multiple_of((group ^ m) * times + at, 16)
    term = lax.dot_general(
        piece,
        r_ref[pl.ds(start, piece.shape[0]), :],
        (((0,), (0,)), ((), ())),
        preferred_element_type=F32,
    )
    s_ref[...] = ((before_ref[...] + term) * inverse_ref[...]).astype(BF16)
    copies = []
    at = 0
    for i, size in enumerate(BLOCKS):
        rows = pl.ds(at * b_ref.shape[0] // 16, size * b_ref.shape[0] // 16)
        at += size
        out_ref[rows, :] = jnp.dot(b_ref[rows, :], s_ref[...], preferred_element_type=F32).astype(BF16)
        copy = pltpu.make_async_copy(out_ref.at[rows], out_hbm.at[rows], sems.at[i])
        copy.start()
        copies.append(copy)
    for copy in copies:
        copy.wait()


def weights(place, pieces, responses, before, inv, basis):
    feats, k = basis.shape
    vox = responses.shape[1]
    return pl.pallas_call(
        functools.partial(weights_kernel, *place),
        in_specs=[VMEM] * 6,
        out_specs=HBM,
        out_shape=jax.ShapeDtypeStruct((feats, vox), BF16),
        scratch_shapes=[
            pltpu.VMEM((k, vox), BF16),
            pltpu.VMEM((feats, vox), BF16),
            pltpu.SemaphoreType.DMA((len(BLOCKS),)),
        ],
        compiler_params=params(24),
        cost_estimate=cost(2 * feats * k * vox, 2 * feats * vox),
        name="weights",
    )(*pieces, responses, before, inv, basis)


def swap(value, group_mask, eig_masks):
    groups, size = lax.axis_size("groups"), lax.axis_size("eig")
    pairs = []
    for g in range(groups):
        for e in range(size):
            mask = eig_masks[half_of(g, e)]
            mask ^= (parity(mask & ~1, EIG_FLIP) + parity(group_mask, GROUP_FLIP)) % 2
            pairs.append((g * size + e, (g ^ group_mask) * size + (e ^ mask)))
    return lax.ppermute(value, ("groups", "eig"), pairs)


def bits(size):
    out = []
    while (1 << len(out)) < size:
        out.append(1 << len(out))
    return out


def orders(size):
    steps = bits(size)[1:]
    turn = [steps[i:] + steps[:i] for i in range(len(steps))]
    return [[turn[0], turn[-1]], [turn[1 % len(steps)], turn[-1]]]


def body(features, responses, basis, eigenvalues, reg_index, subject, alpha_table):
    groups = lax.axis_size("groups")
    total, send, rest, panel = gram_first(features, basis, groups)
    totals, gots = [total], [swap(send, 0, (1, 1))]
    total, send = gram_rest(rest, panel, (send,))
    totals.append(total)
    gots.append(swap(send, 0, (1, 1)))
    sends = [None] * CHAINS
    last = (send,)
    masks = orders(lax.axis_size("eig"))
    count = len(masks[0][0])
    for at in range(count + 1):
        if at == count:
            inv = inverse(alpha_table, reg_index, subject, eigenvalues, last)
            last = (inv,)
        for i in range(CHAINS):
            if at == count:
                sends[i] = add(totals[i], gots[i], last, True)
            else:
                totals[i], sends[i] = add(totals[i], gots[i], last)
                gots[i] = swap(sends[i], 0, [masks[i][half][at] for half in range(2)])
            last = (sends[i],)

    blocks = [sends]
    for bit in bits(groups):
        blocks = blocks + [[swap(piece, bit, (0, 0)) for piece in block] for block in blocks]
    offsets = (0, sends[0].shape[0])
    places = [(m, i) for m in range(groups) for i in range(CHAINS)]
    batches = [places[:CHAINS]] + [[place] for place in places[CHAINS:]]
    total = None
    for batch in batches:
        pieces = []
        for m, i in batch:
            pieces += [blocks[m][i], swap(blocks[m][i], 0, (1, 1))]
        if batch is not batches[-1]:
            total = share([(m, offsets[i]) for m, i in batch], pieces, responses, total)
    (m, i), = batches[-1]
    return weights((m, offsets[i]), pieces, responses, total, inv, panel)


def solution(mesh):
    in_specs = (
        P(None, "eig"),
        P(None, "groups"),
        P("eig", None),
        P(),
        P("groups"),
        P("groups"),
        P(),
    )
    out_specs = P("eig", "groups")
    return jax.shard_map(body, mesh=mesh, in_specs=in_specs, out_specs=out_specs, check_vma=False)
```

```python
import functools

import jax
import jax.numpy as jnp
from jax import lax
from jax.experimental import pallas as pl
from jax.experimental.pallas import tpu as pltpu
from jax.sharding import PartitionSpec as P

F32 = jnp.float32
BF16 = jnp.bfloat16
MIB = 1 << 20
CHAINS = 2
BLOCKS = (1, 2, 2, 2, 2, 2, 2, 2, 1)
EIG_FLIP = 10
GROUP_FLIP = 1
FIRST = 8
ANY = pl.BlockSpec(memory_space=pl.ANY)
HBM = pl.BlockSpec(memory_space=pltpu.HBM)
VMEM = pl.BlockSpec(memory_space=pltpu.VMEM)


def params(mib):
    return pltpu.CompilerParams(vmem_limit_bytes=mib * MIB)


def cost(flops, moved):
    return pl.CostEstimate(flops=flops, bytes_accessed=moved, transcendentals=0)


def in_hbm(value):
    return pltpu.with_memory_space_constraint(value, pltpu.HBM)


def parity(value, mask):
    total = 0
    while mask:
        low = mask & -mask
        total = total + (value // low) % 2
        mask ^= low
    return total % 2


def half_of(group, eig):
    return (parity(eig, EIG_FLIP | 1) + parity(group, GROUP_FLIP)) % 2


def half_index():
    return half_of(lax.axis_index("groups"), lax.axis_index("eig"))


def chain_rows(times):
    first = times * FIRST // 16
    return first, times - first


def split_halves(total, kept_ref, sent_ref):
    half = kept_ref.shape[1]
    low, high = total[:, :half], total[:, half:]
    first = half_index() == 0
    kept_ref[...] = jnp.where(first, low, high)
    sent_ref[...] = jnp.where(first, high, low).astype(sent_ref.dtype)


def gram_first_kernel(f_hbm, b_hbm, kept_ref, sent_ref, rest_ref, b_ref, f_ref, f_sem, b_sem, rest_sem):
    rows, feats = f_ref.shape
    parts = f_sem.shape[0]
    chunk = feats // parts
    more = rest_ref.shape[0]
    start = pl.multiple_of(lax.axis_index("groups") * (rows + more), 16)
    after = pl.multiple_of(start + rows, 16)
    copies = []
    for i in range(parts):
        cols = pl.ds(i * chunk, chunk)
        b_copy = pltpu.make_async_copy(b_hbm.at[cols], b_ref.at[cols], b_sem.at[i])
        f_copy = pltpu.make_async_copy(f_hbm.at[pl.ds(start, rows), cols], f_ref.at[:, cols], f_sem.at[i])
        b_copy.start()
        f_copy.start()
        copies.append((b_copy, f_copy))
    rest_copy = pltpu.make_async_copy(f_hbm.at[pl.ds(after, more)], rest_ref, rest_sem)
    rest_copy.start()
    total = None
    for i, (b_copy, f_copy) in enumerate(copies):
        cols = pl.ds(i * chunk, chunk)
        b_copy.wait()
        f_copy.wait()
        term = jnp.dot(f_ref[:, cols], b_ref[cols, :], preferred_element_type=F32)
        total = term if total is None else total + term
    split_halves(total, kept_ref, sent_ref)
    rest_copy.wait()


def gram_rest_kernel(f_ref, b_ref, *refs):
    kept_ref, sent_ref = refs[-2:]
    split_halves(jnp.dot(f_ref[...], b_ref[...], preferred_element_type=F32), kept_ref, sent_ref)


def gram_first(features, basis, groups):
    times, feats = features.shape
    k = basis.shape[1]
    rows, more = chain_rows(times // groups)
    parts = 2
    return pl.pallas_call(
        gram_first_kernel,
        in_specs=[HBM, HBM],
        out_specs=[VMEM] * 4,
        out_shape=[
            jax.ShapeDtypeStruct((rows, k // 2), F32),
            jax.ShapeDtypeStruct((rows, k // 2), F32),
            jax.ShapeDtypeStruct((more, feats), BF16),
            jax.ShapeDtypeStruct((feats, k), BF16),
        ],
        scratch_shapes=[
            pltpu.VMEM((rows, feats), BF16),
            pltpu.SemaphoreType.DMA((parts,)),
            pltpu.SemaphoreType.DMA((parts,)),
            pltpu.SemaphoreType.DMA,
        ],
        compiler_params=params(12),
        cost_estimate=cost(2 * rows * feats * k, 2 * (rows + k) * feats),
        name="gram_first",
    )(in_hbm(features), in_hbm(basis))


def gram_rest(rest, basis, after):
    rows, feats = rest.shape
    k = basis.shape[1]
    return pl.pallas_call(
        gram_rest_kernel,
        in_specs=[VMEM, VMEM] + [ANY] * len(after),
        out_specs=[VMEM] * 2,
        out_shape=[
            jax.ShapeDtypeStruct((rows, k // 2), F32),
            jax.ShapeDtypeStruct((rows, k // 2), F32),
        ],
        compiler_params=params(8),
        cost_estimate=cost(2 * rows * feats * k, 2 * (rows + k) * feats),
        name="gram_rest",
    )(rest, basis, *after)


def inverse_kernel(table_ref, reg_ref, subject_ref, eig_ref, *refs):
    out_ref = refs[-1]
    subjects, grid = table_ref.shape
    k, vox = out_ref.shape
    picked = lax.broadcasted_iota(jnp.int32, (grid, vox), 0) == reg_ref[...]
    rows = jnp.dot(
        table_ref[...], picked.astype(F32), precision=lax.Precision.HIGHEST, preferred_element_type=F32
    )
    mine = lax.broadcasted_iota(jnp.int32, (subjects, vox), 0) == subject_ref[...]
    alpha = jnp.sum(jnp.where(mine, rows, 0.0), axis=0, keepdims=True)
    side = min(k, 128)
    shape = (side, side)
    diagonal = lax.broadcasted_iota(jnp.int32, shape, 0) == lax.broadcasted_iota(jnp.int32, shape, 1)
    for i in range(k // side):
        at = pl.ds(i * side, side)
        column = jnp.sum(jnp.where(diagonal, eig_ref[:, pl.ds(i * side, side)], 0.0), axis=1, keepdims=True)
        out_ref[at, :] = 1.0 / (column + alpha)


def inverse(alpha_table, reg_index, subject, eigenvalues, after):
    vox = reg_index.shape[0]
    k = eigenvalues.shape[0]
    return pl.pallas_call(
        inverse_kernel,
        in_specs=[VMEM, VMEM, VMEM, VMEM] + [ANY] * len(after),
        out_specs=VMEM,
        out_shape=jax.ShapeDtypeStruct((k, vox), F32),
        compiler_params=params(8),
        cost_estimate=cost(8 * k * vox, 2 * k * vox),
        name="inverse",
    )(alpha_table, reg_index[None, :], subject[None, :], eigenvalues[None, :], *after)


def add_kernel(total_ref, got_ref, *refs):
    out_ref, send_ref = refs[-2:]
    total = total_ref[...] + got_ref[...].astype(F32)
    out_ref[...] = total
    send_ref[...] = total.astype(BF16)


def add_last_kernel(total_ref, got_ref, *refs):
    refs[-1][...] = (total_ref[...] + got_ref[...].astype(F32)).astype(BF16)


def add(total, got, after, last=False):
    shape = total.shape
    both = [jax.ShapeDtypeStruct(shape, F32), jax.ShapeDtypeStruct(shape, BF16)]
    return pl.pallas_call(
        add_last_kernel if last else add_kernel,
        in_specs=[VMEM, VMEM] + [ANY] * len(after),
        out_specs=VMEM if last else [VMEM, VMEM],
        out_shape=both[1] if last else both,
        compiler_params=params(4),
        cost_estimate=cost(4 * 10**9, 12 * total.size),
        name="add",
    )(total, got, *after)


def share_kernel(places, has_sum, finish, *refs):
    n = 2 * len(places)
    r_ref, out_ref = refs[n], refs[-1]
    rest = list(refs[n + 1 : -1])
    group = lax.axis_index("groups")
    first = half_index() == 0
    times = r_ref.shape[0] // lax.axis_size("groups")
    total = rest.pop(0)[...] if has_sum else None
    for i, (m, at) in enumerate(places):
        own, got = refs[2 * i][...], refs[2 * i + 1][...]
        piece = jnp.concatenate([jnp.where(first, own, got), jnp.where(first, got, own)], axis=1)
        start = pl.multiple_of((group ^ m) * times + at, 16)
        term = lax.dot_general(
            piece,
            r_ref[pl.ds(start, piece.shape[0]), :],
            (((0,), (0,)), ((), ())),
            preferred_element_type=F32,
        )
        total = term if total is None else total + term
    if finish:
        total = total * rest.pop(0)[...]
    out_ref[...] = total.astype(out_ref.dtype)


def share(places, pieces, responses, before=None, inv=None):
    rows, k = pieces[0].shape[0], 2 * pieces[0].shape[1]
    vox = responses.shape[1]
    extra = [value for value in (before, inv) if value is not None]
    return pl.pallas_call(
        functools.partial(share_kernel, places, before is not None, inv is not None),
        in_specs=[VMEM] * (len(pieces) + 1 + len(extra)),
        out_specs=VMEM,
        out_shape=jax.ShapeDtypeStruct((k, vox), F32 if inv is None else BF16),
        compiler_params=params(8),
        cost_estimate=cost(2 * len(places) * rows * k * vox, 2 * rows * vox),
        name="share",
    )(*pieces, responses, *extra)


def weights_kernel(m, at, own_ref, got_ref, r_ref, before_ref, inverse_ref, b_ref, out_hbm, s_ref, out_ref, sems):
    group = lax.axis_index("groups")
    first = half_index() == 0
    own, got = own_ref[...], got_ref[...]
    piece = jnp.concatenate([jnp.where(first, own, got), jnp.where(first, got, own)], axis=1)
    times = r_ref.shape[0] // lax.axis_size("groups")
    start = pl.multiple_of((group ^ m) * times + at, 16)
    term = lax.dot_general(
        piece,
        r_ref[pl.ds(start, piece.shape[0]), :],
        (((0,), (0,)), ((), ())),
        preferred_element_type=F32,
    )
    s_ref[...] = ((before_ref[...] + term) * inverse_ref[...]).astype(BF16)
    copies = []
    at = 0
    for i, size in enumerate(BLOCKS):
        rows = pl.ds(at * b_ref.shape[0] // 16, size * b_ref.shape[0] // 16)
        at += size
        out_ref[rows, :] = jnp.dot(b_ref[rows, :], s_ref[...], preferred_element_type=F32).astype(BF16)
        copy = pltpu.make_async_copy(out_ref.at[rows], out_hbm.at[rows], sems.at[i])
        copy.start()
        copies.append(copy)
    for copy in copies:
        copy.wait()


def weights(place, pieces, responses, before, inv, basis):
    feats, k = basis.shape
    vox = responses.shape[1]
    return pl.pallas_call(
        functools.partial(weights_kernel, *place),
        in_specs=[VMEM] * 6,
        out_specs=HBM,
        out_shape=jax.ShapeDtypeStruct((feats, vox), BF16),
        scratch_shapes=[
            pltpu.VMEM((k, vox), BF16),
            pltpu.VMEM((feats, vox), BF16),
            pltpu.SemaphoreType.DMA((len(BLOCKS),)),
        ],
        compiler_params=params(24),
        cost_estimate=cost(2 * feats * k * vox, 2 * feats * vox),
        name="weights",
    )(*pieces, responses, before, inv, basis)


def swap(value, group_mask, eig_masks):
    groups, size = lax.axis_size("groups"), lax.axis_size("eig")
    pairs = []
    for g in range(groups):
        for e in range(size):
            mask = eig_masks[half_of(g, e)]
            mask ^= (parity(mask & ~1, EIG_FLIP) + parity(group_mask, GROUP_FLIP)) % 2
            pairs.append((g * size + e, (g ^ group_mask) * size + (e ^ mask)))
    return lax.ppermute(value, ("groups", "eig"), pairs)


def bits(size):
    out = []
    while (1 << len(out)) < size:
        out.append(1 << len(out))
    return out


def orders(size):
    steps = bits(size)[1:]
    turn = [steps[i:] + steps[:i] for i in range(len(steps))]
    return [[turn[0], turn[-1]], [turn[1 % len(steps)], turn[-1]]]


def body(features, responses, basis, eigenvalues, reg_index, subject, alpha_table):
    groups = lax.axis_size("groups")
    total, send, rest, panel = gram_first(features, basis, groups)
    totals, gots = [total], [swap(send, 0, (1, 1))]
    total, send = gram_rest(rest, panel, (send,))
    totals.append(total)
    gots.append(swap(send, 0, (1, 1)))
    sends = [None] * CHAINS
    last = (send,)
    masks = orders(lax.axis_size("eig"))
    count = len(masks[0][0])
    for at in range(count + 1):
        if at == count:
            inv = inverse(alpha_table, reg_index, subject, eigenvalues, last)
            last = (inv,)
        for i in range(CHAINS):
            if at == count:
                sends[i] = add(totals[i], gots[i], last, True)
            else:
                totals[i], sends[i] = add(totals[i], gots[i], last)
                gots[i] = swap(sends[i], 0, [masks[i][half][at] for half in range(2)])
            last = (sends[i],)

    blocks = [sends]
    for bit in bits(groups):
        blocks = blocks + [[swap(piece, bit, (0, 0)) for piece in block] for block in blocks]
    offsets = (0, sends[0].shape[0])
    places = [(m, i) for m in range(groups) for i in range(CHAINS)]
    batches = [places[:CHAINS]] + [[place] for place in places[CHAINS:]]
    total = None
    for batch in batches:
        pieces = []
        for m, i in batch:
            pieces += [blocks[m][i], swap(blocks[m][i], 0, (1, 1))]
        if batch is not batches[-1]:
            total = share([(m, offsets[i]) for m, i in batch], pieces, responses, total)
    (m, i), = batches[-1]
    return weights((m, offsets[i]), pieces, responses, total, inv, panel)


def solution(mesh):
    in_specs = (
        P(None, "eig"),
        P(None, "groups"),
        P("eig", None),
        P(),
        P("groups"),
        P("groups"),
        P(),
    )
    out_specs = P("eig", "groups")
    return jax.shard_map(body, mesh=mesh, in_specs=in_specs, out_specs=out_specs, check_vma=False)
```

```python
import functools

import jax
import jax.numpy as jnp
from jax import lax
from jax.experimental import pallas as pl
from jax.experimental.pallas import tpu as pltpu
from jax.sharding import PartitionSpec as P

F32 = jnp.float32
BF16 = jnp.bfloat16
MIB = 1 << 20
CHAINS = 2
BLOCKS = (1, 2, 2, 2, 2, 2, 2, 2, 1)
EIG_FLIP = 10
GROUP_FLIP = 1
FIRST = 8
ANY = pl.BlockSpec(memory_space=pl.ANY)
HBM = pl.BlockSpec(memory_space=pltpu.HBM)
VMEM = pl.BlockSpec(memory_space=pltpu.VMEM)


def params(mib):
    return pltpu.CompilerParams(vmem_limit_bytes=mib * MIB)


def cost(flops, moved):
    return pl.CostEstimate(flops=flops, bytes_accessed=moved, transcendentals=0)


def in_hbm(value):
    return pltpu.with_memory_space_constraint(value, pltpu.HBM)


def parity(value, mask):
    total = 0
    while mask:
        low = mask & -mask
        total = total + (value // low) % 2
        mask ^= low
    return total % 2


def half_of(group, eig):
    return (parity(eig, EIG_FLIP | 1) + parity(group, GROUP_FLIP)) % 2


def half_index():
    return half_of(lax.axis_index("groups"), lax.axis_index("eig"))


def chain_rows(times):
    first = times * FIRST // 16
    return first, times - first


def split_halves(total, kept_ref, sent_ref):
    half = kept_ref.shape[1]
    low, high = total[:, :half], total[:, half:]
    first = half_index() == 0
    kept_ref[...] = jnp.where(first, low, high)
    sent_ref[...] = jnp.where(first, high, low).astype(sent_ref.dtype)


def gram_first_kernel(f_hbm, b_hbm, kept_ref, sent_ref, rest_ref, b_ref, f_ref, f_sem, b_sem, rest_sem):
    rows, feats = f_ref.shape
    parts = f_sem.shape[0]
    chunk = feats // parts
    more = rest_ref.shape[0]
    start = pl.multiple_of(lax.axis_index("groups") * (rows + more), 16)
    after = pl.multiple_of(start + rows, 16)
    copies = []
    for i in range(parts):
        cols = pl.ds(i * chunk, chunk)
        b_copy = pltpu.make_async_copy(b_hbm.at[cols], b_ref.at[cols], b_sem.at[i])
        f_copy = pltpu.make_async_copy(f_hbm.at[pl.ds(start, rows), cols], f_ref.at[:, cols], f_sem.at[i])
        b_copy.start()
        f_copy.start()
        copies.append((b_copy, f_copy))
    rest_copy = pltpu.make_async_copy(f_hbm.at[pl.ds(after, more)], rest_ref, rest_sem)
    rest_copy.start()
    total = None
    for i, (b_copy, f_copy) in enumerate(copies):
        cols = pl.ds(i * chunk, chunk)
        b_copy.wait()
        f_copy.wait()
        term = jnp.dot(f_ref[:, cols], b_ref[cols, :], preferred_element_type=F32)
        total = term if total is None else total + term
    split_halves(total, kept_ref, sent_ref)
    rest_copy.wait()


def gram_rest_kernel(f_ref, b_ref, *refs):
    kept_ref, sent_ref = refs[-2:]
    split_halves(jnp.dot(f_ref[...], b_ref[...], preferred_element_type=F32), kept_ref, sent_ref)


def gram_first(features, basis, groups):
    times, feats = features.shape
    k = basis.shape[1]
    rows, more = chain_rows(times // groups)
    parts = 2
    return pl.pallas_call(
        gram_first_kernel,
        in_specs=[HBM, HBM],
        out_specs=[VMEM] * 4,
        out_shape=[
            jax.ShapeDtypeStruct((rows, k // 2), F32),
            jax.ShapeDtypeStruct((rows, k // 2), F32),
            jax.ShapeDtypeStruct((more, feats), BF16),
            jax.ShapeDtypeStruct((feats, k), BF16),
        ],
        scratch_shapes=[
            pltpu.VMEM((rows, feats), BF16),
            pltpu.SemaphoreType.DMA((parts,)),
            pltpu.SemaphoreType.DMA((parts,)),
            pltpu.SemaphoreType.DMA,
        ],
        compiler_params=params(12),
        cost_estimate=cost(2 * rows * feats * k, 2 * (rows + k) * feats),
        name="gram_first",
    )(in_hbm(features), in_hbm(basis))


def gram_rest(rest, basis, after):
    rows, feats = rest.shape
    k = basis.shape[1]
    return pl.pallas_call(
        gram_rest_kernel,
        in_specs=[VMEM, VMEM] + [ANY] * len(after),
        out_specs=[VMEM] * 2,
        out_shape=[
            jax.ShapeDtypeStruct((rows, k // 2), F32),
            jax.ShapeDtypeStruct((rows, k // 2), F32),
        ],
        compiler_params=params(8),
        cost_estimate=cost(2 * rows * feats * k, 2 * (rows + k) * feats),
        name="gram_rest",
    )(rest, basis, *after)


def inverse_kernel(table_ref, reg_ref, subject_ref, eig_ref, *refs):
    out_ref = refs[-1]
    subjects, grid = table_ref.shape
    k, vox = out_ref.shape
    picked = lax.broadcasted_iota(jnp.int32, (grid, vox), 0) == reg_ref[...]
    rows = jnp.dot(
        table_ref[...], picked.astype(F32), precision=lax.Precision.HIGHEST, preferred_element_type=F32
    )
    mine = lax.broadcasted_iota(jnp.int32, (subjects, vox), 0) == subject_ref[...]
    alpha = jnp.sum(jnp.where(mine, rows, 0.0), axis=0, keepdims=True)
    side = min(k, 128)
    shape = (side, side)
    diagonal = lax.broadcasted_iota(jnp.int32, shape, 0) == lax.broadcasted_iota(jnp.int32, shape, 1)
    for i in range(k // side):
        at = pl.ds(i * side, side)
        column = jnp.sum(jnp.where(diagonal, eig_ref[:, pl.ds(i * side, side)], 0.0), axis=1, keepdims=True)
        out_ref[at, :] = 1.0 / (column + alpha)


def inverse(alpha_table, reg_index, subject, eigenvalues, after):
    vox = reg_index.shape[0]
    k = eigenvalues.shape[0]
    return pl.pallas_call(
        inverse_kernel,
        in_specs=[VMEM, VMEM, VMEM, VMEM] + [ANY] * len(after),
        out_specs=VMEM,
        out_shape=jax.ShapeDtypeStruct((k, vox), F32),
        compiler_params=params(8),
        cost_estimate=cost(8 * k * vox, 2 * k * vox),
        name="inverse",
    )(alpha_table, reg_index[None, :], subject[None, :], eigenvalues[None, :], *after)


def add_kernel(total_ref, got_ref, *refs):
    out_ref, send_ref = refs[-2:]
    total = total_ref[...] + got_ref[...].astype(F32)
    out_ref[...] = total
    send_ref[...] = total.astype(BF16)


def add_last_kernel(total_ref, got_ref, *refs):
    refs[-1][...] = (total_ref[...] + got_ref[...].astype(F32)).astype(BF16)


def add(total, got, after, last=False):
    shape = total.shape
    both = [jax.ShapeDtypeStruct(shape, F32), jax.ShapeDtypeStruct(shape, BF16)]
    return pl.pallas_call(
        add_last_kernel if last else add_kernel,
        in_specs=[VMEM, VMEM] + [ANY] * len(after),
        out_specs=VMEM if last else [VMEM, VMEM],
        out_shape=both[1] if last else both,
        compiler_params=params(4),
        cost_estimate=cost(4 * 10**9, 12 * total.size),
        name="add",
    )(total, got, *after)


def share_kernel(places, has_sum, finish, *refs):
    n = 2 * len(places)
    r_ref, out_ref = refs[n], refs[-1]
    rest = list(refs[n + 1 : -1])
    group = lax.axis_index("groups")
    first = half_index() == 0
    times = r_ref.shape[0] // lax.axis_size("groups")
    total = rest.pop(0)[...] if has_sum else None
    for i, (m, at) in enumerate(places):
        own, got = refs[2 * i][...], refs[2 * i + 1][...]
        piece = jnp.concatenate([jnp.where(first, own, got), jnp.where(first, got, own)], axis=1)
        start = pl.multiple_of((group ^ m) * times + at, 16)
        term = lax.dot_general(
            piece,
            r_ref[pl.ds(start, piece.shape[0]), :],
            (((0,), (0,)), ((), ())),
            preferred_element_type=F32,
        )
        total = term if total is None else total + term
    if finish:
        total = total * rest.pop(0)[...]
    out_ref[...] = total.astype(out_ref.dtype)


def share(places, pieces, responses, before=None, inv=None):
    rows, k = pieces[0].shape[0], 2 * pieces[0].shape[1]
    vox = responses.shape[1]
    extra = [value for value in (before, inv) if value is not None]
    return pl.pallas_call(
        functools.partial(share_kernel, places, before is not None, inv is not None),
        in_specs=[VMEM] * (len(pieces) + 1 + len(extra)),
        out_specs=VMEM,
        out_shape=jax.ShapeDtypeStruct((k, vox), F32 if inv is None else BF16),
        compiler_params=params(8),
        cost_estimate=cost(2 * len(places) * rows * k * vox, 2 * rows * vox),
        name="share",
    )(*pieces, responses, *extra)


def weights_kernel(m, at, own_ref, got_ref, r_ref, before_ref, inverse_ref, b_ref, out_hbm, s_ref, out_ref, sems):
    group = lax.axis_index("groups")
    first = half_index() == 0
    own, got = own_ref[...], got_ref[...]
    piece = jnp.concatenate([jnp.where(first, own, got), jnp.where(first, got, own)], axis=1)
    times = r_ref.shape[0] // lax.axis_size("groups")
    start = pl.multiple_of((group ^ m) * times + at, 16)
    term = lax.dot_general(
        piece,
        r_ref[pl.ds(start, piece.shape[0]), :],
        (((0,), (0,)), ((), ())),
        preferred_element_type=F32,
    )
    s_ref[...] = ((before_ref[...] + term) * inverse_ref[...]).astype(BF16)
    copies = []
    at = 0
    for i, size in enumerate(BLOCKS):
        rows = pl.ds(at * b_ref.shape[0] // 16, size * b_ref.shape[0] // 16)
        at += size
        out_ref[rows, :] = jnp.dot(b_ref[rows, :], s_ref[...], preferred_element_type=F32).astype(BF16)
        copy = pltpu.make_async_copy(out_ref.at[rows], out_hbm.at[rows], sems.at[i])
        copy.start()
        copies.append(copy)
    for copy in copies:
        copy.wait()


def weights(place, pieces, responses, before, inv, basis):
    feats, k = basis.shape
    vox = responses.shape[1]
    return pl.pallas_call(
        functools.partial(weights_kernel, *place),
        in_specs=[VMEM] * 6,
        out_specs=HBM,
        out_shape=jax.ShapeDtypeStruct((feats, vox), BF16),
        scratch_shapes=[
            pltpu.VMEM((k, vox), BF16),
            pltpu.VMEM((feats, vox), BF16),
            pltpu.SemaphoreType.DMA((len(BLOCKS),)),
        ],
        compiler_params=params(24),
        cost_estimate=cost(2 * feats * k * vox, 2 * feats * vox),
        name="weights",
    )(*pieces, responses, before, inv, basis)


def swap(value, group_mask, eig_masks):
    groups, size = lax.axis_size("groups"), lax.axis_size("eig")
    pairs = []
    for g in range(groups):
        for e in range(size):
            mask = eig_masks[half_of(g, e)]
            mask ^= (parity(mask & ~1, EIG_FLIP) + parity(group_mask, GROUP_FLIP)) % 2
            pairs.append((g * size + e, (g ^ group_mask) * size + (e ^ mask)))
    return lax.ppermute(value, ("groups", "eig"), pairs)


def bits(size):
    out = []
    while (1 << len(out)) < size:
        out.append(1 << len(out))
    return out


def orders(size):
    steps = bits(size)[1:]
    turn = [steps[i:] + steps[:i] for i in range(len(steps))]
    return [[turn[0], turn[-1]], [turn[1 % len(steps)], turn[-1]]]


def body(features, responses, basis, eigenvalues, reg_index, subject, alpha_table):
    groups = lax.axis_size("groups")
    total, send, rest, panel = gram_first(features, basis, groups)
    totals, gots = [total], [swap(send, 0, (1, 1))]
    total, send = gram_rest(rest, panel, (send,))
    totals.append(total)
    gots.append(swap(send, 0, (1, 1)))
    sends = [None] * CHAINS
    last = (send,)
    masks = orders(lax.axis_size("eig"))
    count = len(masks[0][0])
    for at in range(count + 1):
        if at == 1:
            inv = inverse(alpha_table, reg_index, subject, eigenvalues, last)
            last = (inv,)
        for i in range(CHAINS):
            if at == count:
                sends[i] = add(totals[i], gots[i], last, True)
            else:
                totals[i], sends[i] = add(totals[i], gots[i], last)
                gots[i] = swap(sends[i], 0, [masks[i][half][at] for half in range(2)])
            last = (sends[i],)

    blocks = [sends]
    for bit in bits(groups):
        blocks = blocks + [[swap(piece, bit, (0, 0)) for piece in block] for block in blocks]
    offsets = (0, sends[0].shape[0])
    places = [(m, i) for m in range(groups) for i in range(CHAINS)]
    batches = [places[:CHAINS]] + [[place] for place in places[CHAINS:]]
    total = None
    for batch in batches:
        pieces = []
        for m, i in batch:
            pieces += [blocks[m][i], swap(blocks[m][i], 0, (1, 1))]
        if batch is not batches[-1]:
            total = share([(m, offsets[i]) for m, i in batch], pieces, responses, total)
    (m, i), = batches[-1]
    return weights((m, offsets[i]), pieces, responses, total, inv, panel)


def solution(mesh):
    in_specs = (
        P(None, "eig"),
        P(None, "groups"),
        P("eig", None),
        P(),
        P("groups"),
        P("groups"),
        P(),
    )
    out_specs = P("eig", "groups")
    return jax.shard_map(body, mesh=mesh, in_specs=in_specs, out_specs=out_specs, check_vma=False)
```

```python
import functools

import jax
import jax.numpy as jnp
from jax import lax
from jax.experimental import pallas as pl
from jax.experimental.pallas import tpu as pltpu
from jax.sharding import PartitionSpec as P

F32 = jnp.float32
BF16 = jnp.bfloat16
MIB = 1 << 20
CHAINS = 2
BLOCKS = (1, 3, 4, 4, 3, 1)
EIG_FLIP = 10
GROUP_FLIP = 1
FIRST = 8
ANY = pl.BlockSpec(memory_space=pl.ANY)
HBM = pl.BlockSpec(memory_space=pltpu.HBM)
VMEM = pl.BlockSpec(memory_space=pltpu.VMEM)


def params(mib):
    return pltpu.CompilerParams(vmem_limit_bytes=mib * MIB)


def cost(flops, moved):
    return pl.CostEstimate(flops=flops, bytes_accessed=moved, transcendentals=0)


def in_hbm(value):
    return pltpu.with_memory_space_constraint(value, pltpu.HBM)


def parity(value, mask):
    total = 0
    while mask:
        low = mask & -mask
        total = total + (value // low) % 2
        mask ^= low
    return total % 2


def half_of(group, eig):
    return (parity(eig, EIG_FLIP | 1) + parity(group, GROUP_FLIP)) % 2


def half_index():
    return half_of(lax.axis_index("groups"), lax.axis_index("eig"))


def chain_rows(times):
    first = times * FIRST // 16
    return first, times - first


def split_halves(total, kept_ref, sent_ref):
    half = kept_ref.shape[1]
    low, high = total[:, :half], total[:, half:]
    first = half_index() == 0
    kept_ref[...] = jnp.where(first, low, high)
    sent_ref[...] = jnp.where(first, high, low).astype(sent_ref.dtype)


def gram_first_kernel(f_hbm, b_hbm, kept_ref, sent_ref, rest_ref, b_ref, f_ref, f_sem, b_sem, rest_sem):
    rows, feats = f_ref.shape
    parts = f_sem.shape[0]
    chunk = feats // parts
    more = rest_ref.shape[0]
    start = pl.multiple_of(lax.axis_index("groups") * (rows + more), 16)
    after = pl.multiple_of(start + rows, 16)
    copies = []
    for i in range(parts):
        cols = pl.ds(i * chunk, chunk)
        b_copy = pltpu.make_async_copy(b_hbm.at[cols], b_ref.at[cols], b_sem.at[i])
        f_copy = pltpu.make_async_copy(f_hbm.at[pl.ds(start, rows), cols], f_ref.at[:, cols], f_sem.at[i])
        b_copy.start()
        f_copy.start()
        copies.append((b_copy, f_copy))
    rest_copy = pltpu.make_async_copy(f_hbm.at[pl.ds(after, more)], rest_ref, rest_sem)
    rest_copy.start()
    total = None
    for i, (b_copy, f_copy) in enumerate(copies):
        cols = pl.ds(i * chunk, chunk)
        b_copy.wait()
        f_copy.wait()
        term = jnp.dot(f_ref[:, cols], b_ref[cols, :], preferred_element_type=F32)
        total = term if total is None else total + term
    split_halves(total, kept_ref, sent_ref)
    rest_copy.wait()


def gram_rest_kernel(f_ref, b_ref, *refs):
    kept_ref, sent_ref = refs[-2:]
    split_halves(jnp.dot(f_ref[...], b_ref[...], preferred_element_type=F32), kept_ref, sent_ref)


def gram_first(features, basis, groups):
    times, feats = features.shape
    k = basis.shape[1]
    rows, more = chain_rows(times // groups)
    parts = 2
    return pl.pallas_call(
        gram_first_kernel,
        in_specs=[HBM, HBM],
        out_specs=[VMEM] * 4,
        out_shape=[
            jax.ShapeDtypeStruct((rows, k // 2), F32),
            jax.ShapeDtypeStruct((rows, k // 2), F32),
            jax.ShapeDtypeStruct((more, feats), BF16),
            jax.ShapeDtypeStruct((feats, k), BF16),
        ],
        scratch_shapes=[
            pltpu.VMEM((rows, feats), BF16),
            pltpu.SemaphoreType.DMA((parts,)),
            pltpu.SemaphoreType.DMA((parts,)),
            pltpu.SemaphoreType.DMA,
        ],
        compiler_params=params(12),
        cost_estimate=cost(2 * rows * feats * k, 2 * (rows + k) * feats),
        name="gram_first",
    )(in_hbm(features), in_hbm(basis))


def gram_rest(rest, basis, after):
    rows, feats = rest.shape
    k = basis.shape[1]
    return pl.pallas_call(
        gram_rest_kernel,
        in_specs=[VMEM, VMEM] + [ANY] * len(after),
        out_specs=[VMEM] * 2,
        out_shape=[
            jax.ShapeDtypeStruct((rows, k // 2), F32),
            jax.ShapeDtypeStruct((rows, k // 2), F32),
        ],
        compiler_params=params(8),
        cost_estimate=cost(2 * rows * feats * k, 2 * (rows + k) * feats),
        name="gram_rest",
    )(rest, basis, *after)


def inverse_kernel(table_ref, reg_ref, subject_ref, eig_ref, *refs):
    out_ref = refs[-1]
    subjects, grid = table_ref.shape
    k, vox = out_ref.shape
    picked = lax.broadcasted_iota(jnp.int32, (grid, vox), 0) == reg_ref[...]
    rows = jnp.dot(
        table_ref[...], picked.astype(F32), precision=lax.Precision.HIGHEST, preferred_element_type=F32
    )
    mine = lax.broadcasted_iota(jnp.int32, (subjects, vox), 0) == subject_ref[...]
    alpha = jnp.sum(jnp.where(mine, rows, 0.0), axis=0, keepdims=True)
    side = min(k, 128)
    shape = (side, side)
    diagonal = lax.broadcasted_iota(jnp.int32, shape, 0) == lax.broadcasted_iota(jnp.int32, shape, 1)
    for i in range(k // side):
        at = pl.ds(i * side, side)
        column = jnp.sum(jnp.where(diagonal, eig_ref[:, pl.ds(i * side, side)], 0.0), axis=1, keepdims=True)
        out_ref[at, :] = 1.0 / (column + alpha)


def inverse(alpha_table, reg_index, subject, eigenvalues, after):
    vox = reg_index.shape[0]
    k = eigenvalues.shape[0]
    return pl.pallas_call(
        inverse_kernel,
        in_specs=[VMEM, VMEM, VMEM, VMEM] + [ANY] * len(after),
        out_specs=VMEM,
        out_shape=jax.ShapeDtypeStruct((k, vox), F32),
        compiler_params=params(8),
        cost_estimate=cost(8 * k * vox, 2 * k * vox),
        name="inverse",
    )(alpha_table, reg_index[None, :], subject[None, :], eigenvalues[None, :], *after)


def add_kernel(total_ref, got_ref, *refs):
    out_ref, send_ref = refs[-2:]
    total = total_ref[...] + got_ref[...].astype(F32)
    out_ref[...] = total
    send_ref[...] = total.astype(BF16)


def add_last_kernel(total_ref, got_ref, *refs):
    refs[-1][...] = (total_ref[...] + got_ref[...].astype(F32)).astype(BF16)


def add(total, got, after, last=False):
    shape = total.shape
    both = [jax.ShapeDtypeStruct(shape, F32), jax.ShapeDtypeStruct(shape, BF16)]
    return pl.pallas_call(
        add_last_kernel if last else add_kernel,
        in_specs=[VMEM, VMEM] + [ANY] * len(after),
        out_specs=VMEM if last else [VMEM, VMEM],
        out_shape=both[1] if last else both,
        compiler_params=params(4),
        cost_estimate=cost(4 * 10**9, 12 * total.size),
        name="add",
    )(total, got, *after)


def share_kernel(places, has_sum, finish, *refs):
    n = 2 * len(places)
    r_ref, out_ref = refs[n], refs[-1]
    rest = list(refs[n + 1 : -1])
    group = lax.axis_index("groups")
    first = half_index() == 0
    times = r_ref.shape[0] // lax.axis_size("groups")
    total = rest.pop(0)[...] if has_sum else None
    for i, (m, at) in enumerate(places):
        own, got = refs[2 * i][...], refs[2 * i + 1][...]
        piece = jnp.concatenate([jnp.where(first, own, got), jnp.where(first, got, own)], axis=1)
        start = pl.multiple_of((group ^ m) * times + at, 16)
        term = lax.dot_general(
            piece,
            r_ref[pl.ds(start, piece.shape[0]), :],
            (((0,), (0,)), ((), ())),
            preferred_element_type=F32,
        )
        total = term if total is None else total + term
    if finish:
        total = total * rest.pop(0)[...]
    out_ref[...] = total.astype(out_ref.dtype)


def share(places, pieces, responses, before=None, inv=None):
    rows, k = pieces[0].shape[0], 2 * pieces[0].shape[1]
    vox = responses.shape[1]
    extra = [value for value in (before, inv) if value is not None]
    return pl.pallas_call(
        functools.partial(share_kernel, places, before is not None, inv is not None),
        in_specs=[VMEM] * (len(pieces) + 1 + len(extra)),
        out_specs=VMEM,
        out_shape=jax.ShapeDtypeStruct((k, vox), F32 if inv is None else BF16),
        compiler_params=params(8),
        cost_estimate=cost(2 * len(places) * rows * k * vox, 2 * rows * vox),
        name="share",
    )(*pieces, responses, *extra)


def weights_kernel(m, at, own_ref, got_ref, r_ref, before_ref, inverse_ref, b_ref, out_hbm, s_ref, out_ref, sems):
    group = lax.axis_index("groups")
    first = half_index() == 0
    own, got = own_ref[...], got_ref[...]
    piece = jnp.concatenate([jnp.where(first, own, got), jnp.where(first, got, own)], axis=1)
    times = r_ref.shape[0] // lax.axis_size("groups")
    start = pl.multiple_of((group ^ m) * times + at, 16)
    term = lax.dot_general(
        piece,
        r_ref[pl.ds(start, piece.shape[0]), :],
        (((0,), (0,)), ((), ())),
        preferred_element_type=F32,
    )
    s_ref[...] = ((before_ref[...] + term) * inverse_ref[...]).astype(BF16)
    copies = []
    at = 0
    for i, size in enumerate(BLOCKS):
        rows = pl.ds(at * b_ref.shape[0] // 16, size * b_ref.shape[0] // 16)
        at += size
        out_ref[rows, :] = jnp.dot(b_ref[rows, :], s_ref[...], preferred_element_type=F32).astype(BF16)
        copy = pltpu.make_async_copy(out_ref.at[rows], out_hbm.at[rows], sems.at[i])
        copy.start()
        copies.append(copy)
    for copy in copies:
        copy.wait()


def weights(place, pieces, responses, before, inv, basis):
    feats, k = basis.shape
    vox = responses.shape[1]
    return pl.pallas_call(
        functools.partial(weights_kernel, *place),
        in_specs=[VMEM] * 6,
        out_specs=HBM,
        out_shape=jax.ShapeDtypeStruct((feats, vox), BF16),
        scratch_shapes=[
            pltpu.VMEM((k, vox), BF16),
            pltpu.VMEM((feats, vox), BF16),
            pltpu.SemaphoreType.DMA((len(BLOCKS),)),
        ],
        compiler_params=params(24),
        cost_estimate=cost(2 * feats * k * vox, 2 * feats * vox),
        name="weights",
    )(*pieces, responses, before, inv, basis)


def swap(value, group_mask, eig_masks):
    groups, size = lax.axis_size("groups"), lax.axis_size("eig")
    pairs = []
    for g in range(groups):
        for e in range(size):
            mask = eig_masks[half_of(g, e)]
            mask ^= (parity(mask & ~1, EIG_FLIP) + parity(group_mask, GROUP_FLIP)) % 2
            pairs.append((g * size + e, (g ^ group_mask) * size + (e ^ mask)))
    return lax.ppermute(value, ("groups", "eig"), pairs)


def bits(size):
    out = []
    while (1 << len(out)) < size:
        out.append(1 << len(out))
    return out


def orders(size):
    steps = bits(size)[1:]
    turn = [steps[i:] + steps[:i] for i in range(len(steps))]
    return [[turn[0], turn[-1]], [turn[1 % len(steps)], turn[-1]]]


def body(features, responses, basis, eigenvalues, reg_index, subject, alpha_table):
    groups = lax.axis_size("groups")
    total, send, rest, panel = gram_first(features, basis, groups)
    totals, gots = [total], [swap(send, 0, (1, 1))]
    total, send = gram_rest(rest, panel, (send,))
    totals.append(total)
    gots.append(swap(send, 0, (1, 1)))
    sends = [None] * CHAINS
    last = (send,)
    masks = orders(lax.axis_size("eig"))
    count = len(masks[0][0])
    for at in range(count + 1):
        if at == 1:
            inv = inverse(alpha_table, reg_index, subject, eigenvalues, last)
            last = (inv,)
        for i in range(CHAINS):
            if at == count:
                sends[i] = add(totals[i], gots[i], last, True)
            else:
                totals[i], sends[i] = add(totals[i], gots[i], last)
                gots[i] = swap(sends[i], 0, [masks[i][half][at] for half in range(2)])
            last = (sends[i],)

    blocks = [sends]
    for bit in bits(groups):
        blocks = blocks + [[swap(piece, bit, (0, 0)) for piece in block] for block in blocks]
    offsets = (0, sends[0].shape[0])
    places = [(m, i) for m in range(groups) for i in range(CHAINS)]
    batches = [places[:CHAINS]] + [[place] for place in places[CHAINS:]]
    total = None
    for batch in batches:
        pieces = []
        for m, i in batch:
            pieces += [blocks[m][i], swap(blocks[m][i], 0, (1, 1))]
        if batch is not batches[-1]:
            total = share([(m, offsets[i]) for m, i in batch], pieces, responses, total)
    (m, i), = batches[-1]
    return weights((m, offsets[i]), pieces, responses, total, inv, panel)


def solution(mesh):
    in_specs = (
        P(None, "eig"),
        P(None, "groups"),
        P("eig", None),
        P(),
        P("groups"),
        P("groups"),
        P(),
    )
    out_specs = P("eig", "groups")
    return jax.shard_map(body, mesh=mesh, in_specs=in_specs, out_specs=out_specs, check_vma=False)
```
